512 devices in a mesh: dp: 64 (over x, y, core), mp: 8 (over z).
Axes of the slice: x: 4, y: 8, z: 8, core: 2. Of those that a mesh axis runs over, the one named last changes fastest.
Arguments:
- activations: bfloat16 [32768, 4096], P('dp', 'mp'), may hold values from -30 to 30
- cotangent: bfloat16 [32768, 1024], P('dp', 'mp'), may hold values from -0.125 to 0.125
- block_start: int32 [8, 80], replicated, may hold values from 0 to 127, as said below
- block_owner: int32 [8, 80], replicated, may hold values from 0 to 63, as said below
- first_moment: float32 [8, 64, 4, 4096], P('mp', 'dp'), may hold values from -6 to 6
- block_second: float32 [8, 64, 2], P('mp', 'dp'), may hold values from 0.25 to 4
- master_rows: float32 [8, 64, 4, 4096], P('mp', 'dp'), may hold values from -6 to 6
Outputs:
- new_weight: bfloat16 [1024, 4096], P('mp')
- moment_new: float32 [8, 64, 4, 4096], P('mp', 'dp')
- second_new: float32 [8, 64, 2], P('mp', 'dp')
- master_new: float32 [8, 64, 4, 4096], P('mp', 'dp')
The draws below stay inside these ranges and needn't reach their ends.
Inputs may be any that keep to these rules, and one draw needn't show every extreme that they name: `block_start`: for each head, the first neuron of each of its 80 blocks, increasing from 0; every block holds one or more of the head's 128 neurons. `block_owner`: for each head, a quarter of the ranks own 4 neurons in two blocks, a quarter own 2 neurons in one block, the rest own 1 neuron in one block.
All inputs are finite; a program needn't handle non-finite values.
Results may differ from the reference program's by a relative error of at most 0.001.
Values may be sent and summed in bfloat16 or wider, within the bound.
No kernel may reach another device: no remote copies, remote signals or barrier semaphores. Data moves between devices by JAX's collectives and lax.ppermute only.
A program may use at most 64 MiB of HBM per device.

```python
import math
from functools import partial
import jax
import jax.numpy as jnp
from jax import lax

DW = 4096
HD = 128
KVH = 8
TOKENS = 32768
CAP = 4
NBLK = 80
N_DP = 64


def head_layout(key):
    first_key, second_key, third_key = jax.random.split(key, 3)
    quarter = N_DP // 4
    share = HD // N_DP
    pattern = jnp.concatenate([jnp.full((quarter,), CAP, jnp.int32), jnp.full((quarter,), share, jnp.int32), jnp.full((N_DP - 2 * quarter,), share // 2, jnp.int32)])
    order = jax.random.permutation(first_key, N_DP).astype(jnp.int32)
    counts = pattern[order]
    larger = order < quarter
    first_part = jax.random.randint(second_key, (N_DP,), 1, CAP).astype(jnp.int32)
    sizes_main = jnp.where(larger, first_part, counts)
    large_ids = jnp.argsort(order)[:quarter].astype(jnp.int32)
    sizes_extra = CAP - first_part[large_ids]
    all_owners = jnp.concatenate([jnp.arange(N_DP, dtype=jnp.int32), large_ids])
    all_sizes = jnp.concatenate([sizes_main, sizes_extra])
    shuffle = jax.random.permutation(third_key, NBLK)
    owners_out = all_owners[shuffle]
    sizes_out = all_sizes[shuffle]
    starts = jnp.cumsum(sizes_out) - sizes_out
    return (starts.astype(jnp.int32), owners_out.astype(jnp.int32))


def block_layout(key):
    head_keys = jax.random.split(key, KVH)
    return jax.vmap(head_layout)(head_keys)


def draw_block_start(key, part):
    return block_layout(key)[0]


def draw_block_owner(key, part):
    return block_layout(key)[1]


def draw_activations(key, part):
    key = jax.random.fold_in(key, 7)
    first_key, second_key = jax.random.split(key, 2)
    column_scale = jnp.exp(jax.random.uniform(second_key, (DW,), jnp.float32, math.log(0.3), math.log(3.0)))
    values = jax.random.truncated_normal(first_key, -4.0, 4.0, (TOKENS, DW), jnp.float32) * column_scale[None, :]
    return values.astype(jnp.bfloat16)


def strengthened(entries, key, source, target, shards_of, factor):
    owner, partner = [(jnp.arange(entries.shape[dim]) // (entries.shape[dim] // shards_of)).reshape([-1 if axis == dim else 1 for axis in range(entries.ndim)]) for dim in (source, target)]
    chosen = jax.random.permutation(key, shards_of)[partner]
    strong = (owner == chosen) | (owner == (partner + shards_of // 2) % shards_of)
    return jnp.where(strong, factor * entries, entries)


def levels(stream_key, shape, cuts, low, largest):
    def one(axis_at, blocks):
        draws = jax.random.uniform(jax.random.fold_in(jax.random.fold_in(stream_key, 6), axis_at), (blocks,), jnp.float32, low / len(cuts), largest / len(cuts))
        return jnp.repeat(jnp.exp(draws), shape[axis_at] // blocks).reshape((-1,) + (1,) * (len(shape) - axis_at - 1))

    gain = one(*cuts[0])
    for cut in cuts[1:]:
        gain = gain * one(*cut)
    return gain


def scatter_about(stream_key, shape, scale, bound, shards=(), kind=jnp.bfloat16):
    drawn = jax.random.normal(stream_key, shape, jnp.float32) * scale
    if len(shards) > 0:
        drawn = levels(stream_key, shape, shards, -0.22, 0.18) * drawn
    return jnp.clip(drawn, min=-bound, max=bound).astype(kind)


def gaussian_with(rng, dims, deviation, most, cuts, heavy, kind=jnp.bfloat16):
    entries = deviation * jax.random.normal(rng, dims, jnp.float32)
    if cuts:
        entries = entries * levels(rng, dims, cuts, -0.22, 0.18)
    return jnp.clip(strengthened(entries, jax.random.fold_in(rng, 3), *heavy), -most, most).astype(kind)


def setup_inputs(seed: int = 0) -> dict:
    key_list = jax.random.split(jax.random.key(seed), 8)
    activations = draw_activations(jax.random.fold_in(key_list[7], 71), 0)
    cotangent = gaussian_with(key_list[1], (TOKENS, KVH * HD), 0.0032, 0.125, ((0, 64), (1, 8)), (0, 1, 64, 4.0))
    block_start = draw_block_start(jax.random.fold_in(key_list[7], 71), 0)
    block_owner = draw_block_owner(jax.random.fold_in(key_list[7], 71), 0)
    first_moment = scatter_about(key_list[4], (KVH, N_DP, CAP, DW), 1.0, 6.0, ((0, 8), (1, 64)), jnp.float32)
    block_second = jnp.clip(jnp.exp(math.log(4.0) - 2.7725887 * jax.random.uniform(key_list[5], (KVH, N_DP, 2), jnp.float32) ** levels(key_list[5], (KVH, N_DP, 2), ((0, 8), (1, 64)), -0.2, 0.2)), 0.25, 4.0)
    master_rows = scatter_about(key_list[6], (KVH, N_DP, CAP, DW), 1.0, 6.0, ((0, 8), (1, 64)), jnp.float32)
    return dict(activations=activations, cotangent=cotangent, block_start=block_start, block_owner=block_owner, first_moment=first_moment, block_second=block_second, master_rows=master_rows)


beta_one = 0.9
beta_two = 0.95
learn_rate = 0.05
decay_rate = 0.1
epsilon = 1e-08
fix_one = 1.0 - 0.9 ** 10
fix_two = 1.0 - 0.95 ** 10

def block_tables(starts, owners, owner_count, capacity):
    neuron_ids = jnp.arange(HD, dtype=jnp.int32)
    count_blocks = starts.shape[0]
    block_ids = lax.optimization_barrier(jnp.sum((starts[None, :] <= neuron_ids[:, None]).astype(jnp.int32), axis=1)) - 1
    onehot = block_ids[:, None] == jnp.arange(count_blocks, dtype=jnp.int32)[None, :]
    row_owner = lax.optimization_barrier(jnp.sum(jnp.where(onehot, owners[None, :], 0), axis=1))
    earlier = (row_owner[:, None] == row_owner[None, :]) & (neuron_ids[None, :] < neuron_ids[:, None])
    row_slot = lax.optimization_barrier(jnp.sum(earlier.astype(jnp.int32), axis=1))
    before_blocks = (owners[:, None] == owners[None, :]) & (starts[None, :] < starts[:, None])
    block_rank = lax.optimization_barrier(jnp.sum(before_blocks.astype(jnp.int32), axis=1))
    row_rank = lax.optimization_barrier(jnp.sum(jnp.where(onehot, block_rank[None, :], 0), axis=1))
    target = row_owner * capacity + row_slot
    picker = jnp.arange(owner_count * capacity, dtype=jnp.int32)[:, None] == target[None, :]
    filled = jnp.any(picker, axis=1)
    slot_rank = lax.optimization_barrier(jnp.sum(jnp.where(picker, row_rank[None, :], 0), axis=1))
    assign = filled[:, None] & (slot_rank[:, None] == jnp.arange(2, dtype=jnp.int32)[None, :])
    assign = jnp.transpose(assign.reshape(owner_count, capacity, 2), (0, 2, 1))
    return (picker.astype(jnp.float32), assign.astype(jnp.float32), filled.reshape(owner_count, capacity))

def adam_rows(grad_slots, moment, second, master, assign, filled):
    width = grad_slots.shape[-1]
    row_squares = lax.optimization_barrier(jnp.sum(grad_slots * grad_slots, axis=-1))
    block_sums = jnp.einsum('...qc,...c->...q', assign, row_squares, precision=lax.Precision.HIGHEST)
    block_counts = lax.optimization_barrier(jnp.sum(assign, axis=-1)) * width
    block_used = block_counts > 0.0
    block_mean = block_sums / jnp.maximum(block_counts, 1.0)
    second_new = jnp.where(block_used, beta_two * second + (1.0 - beta_two) * block_mean, 0.0)
    slot_second = jnp.einsum('...qc,...q->...c', assign, second_new, precision=lax.Precision.HIGHEST)
    slot_second = jnp.where(filled, slot_second, 1.0)
    moment_new = jnp.where(filled[..., None], beta_one * moment + (1.0 - beta_one) * grad_slots, 0.0)
    update = moment_new / fix_one / (jnp.sqrt(slot_second / fix_two)[..., None] + epsilon)
    master_new = jnp.where(filled[..., None], master - learn_rate * (update + decay_rate * master), 0.0)
    return (moment_new, second_new, master_new)

def reference(activations, cotangent, block_start, block_owner, first_moment, block_second, master_rows):
    owner_count = first_moment.shape[1]
    capacity = first_moment.shape[2]
    width = first_moment.shape[3]
    heads_all = first_moment.shape[0]
    make = partial(block_tables, owner_count=owner_count, capacity=capacity)
    pickers, assigns, filleds = jax.vmap(make)(block_start, block_owner)
    gradient = jnp.dot(cotangent.T, activations, preferred_element_type=jnp.float32).reshape(heads_all, HD, width)
    owner_grad = jnp.einsum('hcd,hdf->hcf', pickers, gradient, precision=lax.Precision.HIGHEST)
    owner_grad = owner_grad.reshape(heads_all, owner_count, capacity, width)
    moment_new, second_new, master_new = adam_rows(owner_grad, first_moment, block_second, master_rows, assigns, filleds)
    flat_master = master_new.reshape(heads_all, owner_count * capacity, width)
    new_weight = jnp.einsum('hcr,hcf->hrf', pickers, flat_master, precision=lax.Precision.HIGHEST)
    new_weight = new_weight.reshape(heads_all * HD, width).astype(jnp.bfloat16)
    return (new_weight, moment_new, second_new, master_new)
```

```python
from functools import partial

import jax
import jax.numpy as jnp
from jax import lax
from jax.sharding import Mesh, PartitionSpec as P

HD = 128
GRID = (4, 8, 2)


beta_one = 0.9
beta_two = 0.95
learn_rate = 0.05
decay_rate = 0.1
epsilon = 1e-08
fix_one = 1.0 - 0.9**10
fix_two = 1.0 - 0.95**10


def block_tables(starts, owners, capacity):
    neuron_ids = jnp.arange(HD, dtype=jnp.int32)
    count_blocks = starts.shape[0]
    block_ids = jnp.sum((starts[None, :] <= neuron_ids[:, None]).astype(jnp.int32), axis=1) - 1
    onehot = block_ids[:, None] == jnp.arange(count_blocks, dtype=jnp.int32)[None, :]
    row_owner = jnp.sum(jnp.where(onehot, owners[None, :], 0), axis=1)
    earlier = (row_owner[:, None] == row_owner[None, :]) & (
        neuron_ids[None, :] < neuron_ids[:, None]
    )
    row_slot = jnp.sum(earlier.astype(jnp.int32), axis=1)
    before_blocks = (owners[:, None] == owners[None, :]) & (starts[None, :] < starts[:, None])
    block_rank = jnp.sum(before_blocks.astype(jnp.int32), axis=1)
    row_rank = jnp.sum(jnp.where(onehot, block_rank[None, :], 0), axis=1)
    return row_owner * capacity + row_slot, row_rank


def adam_rows(grad_slots, moment, second, master, assign, filled):
    width = grad_slots.shape[-1]
    row_squares = jnp.sum(grad_slots * grad_slots, axis=-1)
    block_sums = jnp.sum(assign * row_squares[None, :], axis=-1)
    block_counts = jnp.sum(assign, axis=-1) * width
    block_used = block_counts > 0.0
    block_mean = block_sums / jnp.maximum(block_counts, 1.0)
    second_new = jnp.where(block_used, beta_two * second + (1.0 - beta_two) * block_mean, 0.0)
    slot_second = jnp.sum(assign * second_new[:, None], axis=0)
    slot_second = jnp.where(filled, slot_second, 1.0)
    moment_new = jnp.where(
        filled[..., None], beta_one * moment + (1.0 - beta_one) * grad_slots, 0.0
    )
    update = moment_new / fix_one / (jnp.sqrt(slot_second / fix_two)[..., None] + epsilon)
    master_new = jnp.where(
        filled[..., None], master - learn_rate * (update + decay_rate * master), 0.0
    )
    return (moment_new, second_new, master_new)


SWAP = [(0, 1), (1, 0)]


def body(activations, cotangent, block_start, block_owner, first_moment, block_second, master_rows):
    nx, ny, nc = GRID
    heads, capacity, width = block_start.shape[0], first_moment.shape[2], first_moment.shape[3]
    chips, slots = nx * ny, nx * ny * nc * capacity
    core, head_here = lax.axis_index("c"), lax.axis_index("z")
    owner_here = (lax.axis_index("x") * ny + lax.axis_index("y")) * nc + core
    half = activations.shape[1] // nc

    cot_here = lax.all_gather(cotangent, "z", axis=0)
    act_here = lax.dynamic_slice_in_dim(activations, core * half, half, 1)
    act_give = lax.dynamic_slice_in_dim(activations, (1 - core) * half, half, 1)
    act_other = lax.ppermute(act_give, "c", SWAP)
    cot_other = lax.ppermute(cot_here, "c", SWAP)

    target, row_rank = jax.vmap(partial(block_tables, capacity=capacity))(block_start, block_owner)
    picker = jnp.arange(slots, dtype=jnp.int32)[None, :, None] == target[:, None, :]
    pick = picker.astype(jnp.bfloat16)

    def part(cot, act):
        wide = jnp.einsum("htn,hsn->hts", cot, pick, preferred_element_type=jnp.float32)
        wide = wide.astype(jnp.bfloat16)
        return jnp.einsum("hts,tf->hsf", wide, act, preferred_element_type=jnp.float32)

    padded = part(cot_here, act_here) + part(cot_other, act_other)
    padded = padded.reshape(heads, chips, nc * capacity, half)
    send = jnp.transpose(padded * 0.5, (1, 0, 2, 3)).astype(jnp.float16)
    send = send.reshape(chips * heads, nc * capacity, half)
    got = lax.all_to_all(send, ("x", "y", "z"), 0, 0, tiled=True)
    got = got.reshape(chips, heads, nc * capacity, half).astype(jnp.float32)
    summed = jnp.sum(got, axis=0) * 2.0

    keep = lax.dynamic_slice_in_dim(summed, core * capacity, capacity, 1)
    give = lax.dynamic_slice_in_dim(summed, (1 - core) * capacity, capacity, 1)
    take = lax.ppermute(give, "c", SWAP)
    first = jnp.where(core == 0, keep, take)
    later = jnp.where(core == 0, take, keep)
    grad_slots = jnp.stack([first, later], axis=1)
    grad_slots = jnp.transpose(grad_slots, (2, 0, 1, 3)).reshape(capacity, width)

    target_here = lax.dynamic_index_in_dim(target, head_here, 0, keepdims=False)
    rank_here = lax.dynamic_index_in_dim(row_rank, head_here, 0, keepdims=False)
    slot_ids = owner_here * capacity + jnp.arange(capacity, dtype=jnp.int32)
    mine = slot_ids[:, None] == target_here[None, :]
    filled_here = jnp.any(mine, axis=1)
    slot_rank = jnp.sum(jnp.where(mine, rank_here[None, :], 0), axis=1)
    assign_here = filled_here[None, :] & (
        slot_rank[None, :] == jnp.arange(2, dtype=jnp.int32)[:, None]
    )
    moment_new, second_new, master_new = adam_rows(
        grad_slots,
        first_moment[0, 0],
        block_second[0, 0],
        master_rows[0, 0],
        assign_here.astype(jnp.float32),
        filled_here,
    )

    rows = master_new.astype(jnp.bfloat16)
    rows = lax.all_to_all(jnp.broadcast_to(rows[None], (ny,) + rows.shape), "y", 0, 0, tiled=True)
    rows = lax.all_to_all(jnp.broadcast_to(rows[None], (nx,) + rows.shape), "x", 0, 0, tiled=True)
    rows = rows.reshape(chips * capacity, width)
    rows_other = lax.ppermute(rows, "c", SWAP)
    pick_here = lax.dynamic_index_in_dim(pick, head_here, 0, keepdims=False)
    pick_here = pick_here.reshape(chips, nc, capacity, HD)
    pick_own = lax.dynamic_index_in_dim(pick_here, core, 1, keepdims=False)
    pick_off = lax.dynamic_index_in_dim(pick_here, 1 - core, 1, keepdims=False)
    place = partial(jnp.einsum, "sr,sf->rf", preferred_element_type=jnp.float32)
    new_weight = place(pick_own.reshape(-1, HD), rows) + place(pick_off.reshape(-1, HD), rows_other)
    return (
        new_weight.astype(jnp.bfloat16),
        moment_new[None, None],
        second_new[None, None],
        master_new[None, None],
    )


def solution(mesh):
    dp = ("x", "y", "c")
    fine = Mesh(mesh.devices.reshape(GRID + (-1,)), dp + ("z",))
    return jax.shard_map(
        body,
        mesh=fine,
        in_specs=(
            P(dp, "z"),
            P(dp, "z"),
            P(),
            P(),
            P("z", dp, None, None),
            P("z", dp, None),
            P("z", dp, None, None),
        ),
        out_specs=(
            P("z", None),
            P("z", dp, None, None),
            P("z", dp, None),
            P("z", dp, None, None),
        ),
        check_vma=False,
    )
```

```python
from functools import partial

import jax
import jax.numpy as jnp
from jax import lax
from jax.experimental import pallas as pl
from jax.experimental.pallas import tpu as pltpu
from jax.sharding import Mesh, PartitionSpec as P

HD = 128
GRID = (4, 8, 2)
PAIR = 2
CUT = 4


beta_one = 0.9
beta_two = 0.95
learn_rate = 0.05
decay_rate = 0.1
epsilon = 1e-08
fix_one = 1.0 - 0.9**10
fix_two = 1.0 - 0.95**10


def block_tables(starts, owners, capacity):
    neuron_ids = jnp.arange(HD, dtype=jnp.int32)
    count_blocks = starts.shape[0]
    block_ids = jnp.sum((starts[None, :] <= neuron_ids[:, None]).astype(jnp.int32), axis=1) - 1
    onehot = block_ids[:, None] == jnp.arange(count_blocks, dtype=jnp.int32)[None, :]
    row_owner = jnp.sum(jnp.where(onehot, owners[None, :], 0), axis=1)
    earlier = (row_owner[:, None] == row_owner[None, :]) & (
        neuron_ids[None, :] < neuron_ids[:, None]
    )
    row_slot = jnp.sum(earlier.astype(jnp.int32), axis=1)
    before_blocks = (owners[:, None] == owners[None, :]) & (starts[None, :] < starts[:, None])
    block_rank = jnp.sum(before_blocks.astype(jnp.int32), axis=1)
    row_rank = jnp.sum(jnp.where(onehot, block_rank[None, :], 0), axis=1)
    return row_owner * capacity + row_slot, row_rank


def adam_rows(grad_slots, moment, second, master, assign, filled):
    width = grad_slots.shape[-1]
    row_squares = jnp.sum(grad_slots * grad_slots, axis=-1)
    block_sums = jnp.sum(assign * row_squares[None, :], axis=-1)
    block_counts = jnp.sum(assign, axis=-1) * width
    block_used = block_counts > 0.0
    block_mean = block_sums / jnp.maximum(block_counts, 1.0)
    second_new = jnp.where(block_used, beta_two * second + (1.0 - beta_two) * block_mean, 0.0)
    slot_second = jnp.sum(assign * second_new[:, None], axis=0)
    slot_second = jnp.where(filled, slot_second, 1.0)
    moment_new = jnp.where(
        filled[..., None], beta_one * moment + (1.0 - beta_one) * grad_slots, 0.0
    )
    update = moment_new / fix_one / (jnp.sqrt(slot_second / fix_two)[..., None] + epsilon)
    master_new = jnp.where(
        filled[..., None], master - learn_rate * (update + decay_rate * master), 0.0
    )
    return (moment_new, second_new, master_new)


SWAP = [(0, 1), (1, 0)]


def copies_to_all(block, axis):
    count = lax.axis_size(axis)
    return lax.all_to_all(jnp.broadcast_to(block[None], (count,) + block.shape), axis, 0, 0, tiled=True)


def gradient_kernel(target_ref, cot_here_ref, cot_other_ref, act_here_ref, act_other_ref, out_ref):
    tokens = (((0,), (0,)), ((), ()))
    grad = lax.dot_general(
        cot_here_ref[0], act_here_ref[...], tokens, preferred_element_type=jnp.float32
    ) + lax.dot_general(
        cot_other_ref[0], act_other_ref[...], tokens, preferred_element_type=jnp.float32
    )
    high = grad.astype(jnp.bfloat16)
    low = (grad - high.astype(jnp.float32)).astype(jnp.bfloat16)
    chips, rows, half = out_ref.shape[0], out_ref.shape[2] // 2, out_ref.shape[3]
    slot = lax.broadcasted_iota(jnp.int32, (chips * rows, HD), 0)
    pick = jnp.where(slot == target_ref[0], 0.5, 0.0).astype(jnp.bfloat16)
    padded = jnp.dot(pick, high, preferred_element_type=jnp.float32) + jnp.dot(
        pick, low, preferred_element_type=jnp.float32
    )
    parts = [padded[:, i * half : (i + 1) * half].reshape(chips, rows, half) for i in range(2)]
    out_ref[:, 0] = jnp.concatenate(parts, axis=1).astype(out_ref.dtype)


def padded_gradient(target, cot_here, cot_other, act_here, act_other, chips, rows):
    heads, tokens, _ = cot_here.shape
    features = act_here.shape[1]
    cot = pl.BlockSpec((1, tokens, HD), lambda h: (h, 0, 0))
    act = pl.BlockSpec((tokens, features), lambda h: (0, 0))
    shape = (chips, heads, 2 * rows, features // 2)
    return pl.pallas_call(
        gradient_kernel,
        grid=(heads,),
        in_specs=[pl.BlockSpec((1, 1, HD), lambda h: (h, 0, 0)), cot, cot, act, act],
        out_specs=pl.BlockSpec((chips, 1) + shape[2:], lambda h: (0, h, 0, 0)),
        out_shape=jax.ShapeDtypeStruct(shape, jnp.float32),
        compiler_params=pltpu.CompilerParams(vmem_limit_bytes=32 * 2**20),
    )(target[:, None, :], cot_here, cot_other, act_here, act_other)


def weight_kernel(target_ref, key_here_ref, key_other_ref, here_ref, other_ref, out_ref):
    want = target_ref[...] * CUT + pl.program_id(0)
    pick_here = jnp.where(want == key_here_ref[...], 1.0, 0.0).astype(jnp.bfloat16)
    pick_other = jnp.where(want == key_other_ref[...], 1.0, 0.0).astype(jnp.bfloat16)
    rows = jnp.dot(pick_here, here_ref[...], preferred_element_type=jnp.float32)
    rows += jnp.dot(pick_other, other_ref[...], preferred_element_type=jnp.float32)
    out_ref[...] = rows.astype(jnp.bfloat16)


def place_rows(target, key_here, key_other, here, other):
    count, piece = here.shape
    whole = lambda shape: pl.BlockSpec(shape, lambda j: (0, 0))
    return pl.pallas_call(
        weight_kernel,
        grid=(CUT,),
        in_specs=[whole((HD, 1)), whole((1, count)), whole((1, count))] + [whole((count, piece))] * 2,
        out_specs=pl.BlockSpec((HD, piece), lambda j: (0, j)),
        out_shape=jax.ShapeDtypeStruct((HD, CUT * piece), jnp.bfloat16),
        compiler_params=pltpu.CompilerParams(vmem_limit_bytes=32 * 2**20),
    )(target[:, None], key_here[None, :], key_other[None, :], here, other)


def body(activations, cotangent, block_start, block_owner, first_moment, block_second, master_rows):
    nx, ny, nc = GRID
    capacity, width = first_moment.shape[2], first_moment.shape[3]
    chips, rows = nx * ny, nc * capacity
    core, side, pair = lax.axis_index("c"), lax.axis_index("zl"), lax.axis_index("zh")
    pairs = lax.axis_size("zh")
    chip = lax.axis_index("x") * ny + lax.axis_index("y")
    owner_here = chip * nc + core
    features = activations.shape[1]

    act_pair = lax.ppermute(activations, "zl", SWAP)
    cot_here = copies_to_all(cotangent, "zh")
    own = core == side
    act_here = jnp.where(own, activations, act_pair)
    act_other = lax.ppermute(jnp.where(own, act_pair, activations), "c", SWAP)
    cot_other = lax.ppermute(cot_here, "c", SWAP)

    def of_side(table):
        return lax.dynamic_index_in_dim(table.reshape(pairs, PAIR, -1), side, 1, keepdims=False)

    target, row_rank = jax.vmap(partial(block_tables, capacity=capacity))(
        of_side(block_start), of_side(block_owner)
    )
    target_here = lax.dynamic_index_in_dim(target, pair, 0, keepdims=False)
    rank_here = lax.dynamic_index_in_dim(row_rank, pair, 0, keepdims=False)
    slot_ids = owner_here * capacity + jnp.arange(capacity, dtype=jnp.int32)
    mine = slot_ids[:, None] == target_here[None, :]
    filled_here = jnp.any(mine, axis=1)
    slot_rank = jnp.sum(jnp.where(mine, rank_here[None, :], 0), axis=1)
    assign_here = filled_here[None, :] & (
        slot_rank[None, :] == jnp.arange(2, dtype=jnp.int32)[:, None]
    )

    send = padded_gradient(target, cot_here, cot_other, act_here, act_other, chips, rows)
    send = send.astype(jnp.float16).reshape(nx, ny * pairs, 2 * rows, features // 2)
    got = lax.all_to_all(send, "x", 0, 0, tiled=True)
    send = jnp.sum(got.astype(jnp.float32), axis=0).astype(jnp.float16)
    got = lax.all_to_all(send, ("y", "zh"), 0, 0, tiled=True)
    got = got.reshape(ny, pairs, 2, nc, capacity, features // 2)
    summed = jnp.sum(got.astype(jnp.float32), axis=0) * 2.0

    keep = lax.dynamic_index_in_dim(summed, core, 2, keepdims=False)
    give = lax.dynamic_index_in_dim(summed, 1 - core, 2, keepdims=False)
    take = lax.ppermute(give, "c", SWAP)
    even = jnp.where(core == 0, keep, take)
    odd = jnp.where(core == 0, take, keep)
    grad_slots = jnp.stack([even, odd], axis=1)
    grad_slots = jnp.transpose(grad_slots, (3, 0, 1, 2, 4)).reshape(capacity, width)
    moment_new, second_new, master_new = adam_rows(
        grad_slots,
        first_moment[0, 0],
        block_second[0, 0],
        master_rows[0, 0],
        assign_here.astype(jnp.float32),
        filled_here,
    )

    low = master_new.astype(jnp.bfloat16).reshape(capacity * CUT, width // CUT)
    low = copies_to_all(copies_to_all(low, "y"), "x").reshape(-1, width // CUT)
    low_other = lax.ppermute(low, "c", SWAP)
    row = jnp.arange(low.shape[0], dtype=jnp.int32)
    from_chip, piece = row // (capacity * CUT), row % (capacity * CUT)
    key_here = (from_chip * nc + core) * capacity * CUT + piece
    key_other = (from_chip * nc + 1 - core) * capacity * CUT + piece
    new_weight = place_rows(target_here, key_here, key_other, low, low_other)
    return (new_weight, moment_new[None, None], second_new[None, None], master_new[None, None])


def solution(mesh):
    dp, mp = ("x", "y", "c"), ("zh", "zl")
    fine = Mesh(mesh.devices.reshape(GRID + (-1, PAIR)), dp + mp)
    return jax.shard_map(
        body,
        mesh=fine,
        in_specs=(
            P(dp, mp),
            P(dp, mp),
            P(),
            P(),
            P(mp, dp, None, None),
            P(mp, dp, None),
            P(mp, dp, None, None),
        ),
        out_specs=(
            P(mp, None),
            P(mp, dp, None, None),
            P(mp, dp, None),
            P(mp, dp, None, None),
        ),
        check_vma=False,
    )
```

```python
from functools import partial

import jax
import jax.numpy as jnp
from jax import lax
from jax.experimental import pallas as pl
from jax.experimental.pallas import tpu as pltpu
from jax.sharding import Mesh, PartitionSpec as P

HD = 128
GRID = (4, 8, 2)
PAIR = 2
CUT = 2


beta_one = 0.9
beta_two = 0.95
learn_rate = 0.05
decay_rate = 0.1
epsilon = 1e-08
fix_one = 1.0 - 0.9**10
fix_two = 1.0 - 0.95**10


def block_tables(starts, owners, capacity):
    neuron_ids = jnp.arange(HD, dtype=jnp.int32)
    count_blocks = starts.shape[0]
    block_ids = jnp.sum((starts[None, :] <= neuron_ids[:, None]).astype(jnp.int32), axis=1) - 1
    onehot = block_ids[:, None] == jnp.arange(count_blocks, dtype=jnp.int32)[None, :]
    row_owner = jnp.sum(jnp.where(onehot, owners[None, :], 0), axis=1)
    earlier = (row_owner[:, None] == row_owner[None, :]) & (
        neuron_ids[None, :] < neuron_ids[:, None]
    )
    row_slot = jnp.sum(earlier.astype(jnp.int32), axis=1)
    before_blocks = (owners[:, None] == owners[None, :]) & (starts[None, :] < starts[:, None])
    block_rank = jnp.sum(before_blocks.astype(jnp.int32), axis=1)
    row_rank = jnp.sum(jnp.where(onehot, block_rank[None, :], 0), axis=1)
    return row_owner * capacity + row_slot, row_rank


def adam_rows(grad_slots, moment, second, master, assign, filled):
    width = grad_slots.shape[-1]
    row_squares = jnp.sum(grad_slots * grad_slots, axis=-1)
    block_sums = jnp.sum(assign * row_squares[None, :], axis=-1)
    block_counts = jnp.sum(assign, axis=-1) * width
    block_used = block_counts > 0.0
    block_mean = block_sums / jnp.maximum(block_counts, 1.0)
    second_new = jnp.where(block_used, beta_two * second + (1.0 - beta_two) * block_mean, 0.0)
    slot_second = jnp.sum(assign * second_new[:, None], axis=0)
    slot_second = jnp.where(filled, slot_second, 1.0)
    moment_new = jnp.where(
        filled[..., None], beta_one * moment + (1.0 - beta_one) * grad_slots, 0.0
    )
    update = moment_new / fix_one / (jnp.sqrt(slot_second / fix_two)[..., None] + epsilon)
    master_new = jnp.where(
        filled[..., None], master - learn_rate * (update + decay_rate * master), 0.0
    )
    return (moment_new, second_new, master_new)


SWAP = [(0, 1), (1, 0)]


def copies_to_all(block, axis):
    count = lax.axis_size(axis)
    return lax.all_to_all(jnp.broadcast_to(block[None], (count,) + block.shape), axis, 0, 0, tiled=True)


TOKEN_DOT = (((0,), (0,)), ((), ()))
PARAMS = pltpu.CompilerParams(vmem_limit_bytes=32 * 2**20)


def cost(flops, moved):
    return pl.CostEstimate(flops=flops, bytes_accessed=moved, transcendentals=0)


def first_kernel(cot_ref, act_ref, out_ref):
    out_ref[0] = lax.dot_general(
        cot_ref[0], act_ref[...], TOKEN_DOT, preferred_element_type=jnp.float32
    )


def padded_kernel(target_ref, first_ref, cot_ref, act_ref, out_ref):
    grad = first_ref[0] + lax.dot_general(
        cot_ref[0], act_ref[...], TOKEN_DOT, preferred_element_type=jnp.float32
    )
    high = grad.astype(jnp.bfloat16)
    low = (grad - high.astype(jnp.float32)).astype(jnp.bfloat16)
    chips, cores, _, rows, half = out_ref.shape
    capacity = rows // 2
    row = lax.broadcasted_iota(jnp.int32, (chips * cores * rows, HD), 0)
    slot = row // rows * capacity + row % capacity
    taken = slot == target_ref[0]
    padded = jnp.zeros((chips * cores * rows, half), jnp.float32)
    for part in range(2):
        pick = jnp.where(taken & (row // capacity % 2 == part), 0.5, 0.0).astype(jnp.bfloat16)
        span = slice(part * half, (part + 1) * half)
        padded += jnp.dot(pick, high[:, span], preferred_element_type=jnp.float32)
        padded += jnp.dot(pick, low[:, span], preferred_element_type=jnp.float32)
    out_ref[:, :, 0] = padded.reshape(chips, cores, rows, half)


def padded_gradient(target, cot_here, cot_other, act_here, act_other, chips, cores, capacity):
    heads, tokens, _ = cot_here.shape
    features = act_here.shape[1]
    cot = pl.BlockSpec((1, tokens, HD), lambda h: (h, 0, 0))
    act = pl.BlockSpec((tokens, features), lambda h: (0, 0))
    grad = pl.BlockSpec((1, HD, features), lambda h: (h, 0, 0))
    first = pl.pallas_call(
        first_kernel,
        grid=(heads,),
        in_specs=[cot, act],
        out_specs=grad,
        out_shape=jax.ShapeDtypeStruct((heads, HD, features), jnp.float32),
        compiler_params=PARAMS,
        cost_estimate=cost(2 * heads * tokens * HD * features, 2 * 2**20),
    )(cot_here, act_here)
    tail = (2 * capacity, features // 2)
    return pl.pallas_call(
        padded_kernel,
        grid=(heads,),
        in_specs=[pl.BlockSpec((1, 1, HD), lambda h: (h, 0, 0)), grad, cot, act],
        out_specs=pl.BlockSpec((chips, cores, 1) + tail, lambda h: (0, 0, h, 0, 0)),
        out_shape=jax.ShapeDtypeStruct((chips, cores, heads) + tail, jnp.float32),
        compiler_params=PARAMS,
        cost_estimate=cost(4 * heads * tokens * HD * features, 4 * 2**20),
    )(target[:, None, :], first, cot_other, act_other)


def place_kernel(target_ref, key_ref, rows_ref, *refs):
    want = target_ref[...] * CUT + pl.program_id(0)
    pick = jnp.where(want == key_ref[...], 1.0, 0.0).astype(jnp.bfloat16)
    placed = jnp.dot(pick, rows_ref[...], preferred_element_type=jnp.float32)
    for ref in refs[:-1]:
        placed += ref[...].astype(jnp.float32)
    refs[-1][...] = placed.astype(jnp.bfloat16)


def place_rows(target, key, rows, *placed):
    count, piece = rows.shape
    whole = lambda shape: pl.BlockSpec(shape, lambda j: (0, 0))
    piece_spec = pl.BlockSpec((HD, piece), lambda j: (0, j))
    return pl.pallas_call(
        place_kernel,
        grid=(CUT,),
        in_specs=[whole((HD, 1)), whole((1, count)), whole((count, piece))] + [piece_spec] * len(placed),
        out_specs=piece_spec,
        out_shape=jax.ShapeDtypeStruct((HD, CUT * piece), jnp.bfloat16),
        compiler_params=PARAMS,
        cost_estimate=cost(2 * CUT * HD * count * piece, 2 * 2**20),
    )(target[:, None], key[None, :], rows, *placed)


FIRST_HAND = [(0, 1), (3, 2), (2, 0), (1, 3)]
SECOND_HAND = [(2, 1), (1, 2)]


def body(activations, cotangent, block_start, block_owner, first_moment, block_second, master_rows):
    nx, ny, nc = GRID
    capacity, width = first_moment.shape[2], first_moment.shape[3]
    chips = nx * ny
    core, side, pair = lax.axis_index("c"), lax.axis_index("zl"), lax.axis_index("zh")
    pairs = lax.axis_size("zh")
    chip = lax.axis_index("x") * ny + lax.axis_index("y")
    owner_here = chip * nc + core
    half = activations.shape[1] // 2

    cot_here = copies_to_all(cotangent, "zh")
    hand_one = lax.ppermute(activations, ("c", "zl"), FIRST_HAND)
    hand_two = lax.ppermute(activations, ("c", "zl"), SECOND_HAND)
    act_here = jnp.where(core == side, activations, hand_one)
    act_other = jnp.where(core == side, hand_one, hand_two)
    cot_other = lax.ppermute(cot_here, "c", SWAP)

    def of_side(table):
        return lax.dynamic_index_in_dim(table.reshape(pairs, PAIR, -1), side, 1, keepdims=False)

    target, row_rank = jax.vmap(partial(block_tables, capacity=capacity))(
        of_side(block_start), of_side(block_owner)
    )
    target_here = lax.dynamic_index_in_dim(target, pair, 0, keepdims=False)
    rank_here = lax.dynamic_index_in_dim(row_rank, pair, 0, keepdims=False)
    slot_ids = owner_here * capacity + jnp.arange(capacity, dtype=jnp.int32)
    mine = slot_ids[:, None] == target_here[None, :]
    filled_here = jnp.any(mine, axis=1)
    slot_rank = jnp.sum(jnp.where(mine, rank_here[None, :], 0), axis=1)
    assign_here = filled_here[None, :] & (
        slot_rank[None, :] == jnp.arange(2, dtype=jnp.int32)[:, None]
    )

    send = padded_gradient(
        target, cot_here, cot_other, act_here, act_other, chips, nc, capacity
    ).astype(jnp.float16)
    send = send.reshape(nx, ny * nc * pairs, 2 * capacity, half)
    got = lax.all_to_all(send, "x", 0, 0, tiled=True)
    send = jnp.sum(got.astype(jnp.float32), axis=0).astype(jnp.float16)
    got = lax.all_to_all(send, ("y", "c", "zh"), 0, 0, tiled=True)
    got = got.reshape(ny, nc, pairs, 2, capacity, half)
    summed = jnp.sum(got.astype(jnp.float32), axis=0) * 2.0
    grad_slots = jnp.transpose(summed, (3, 1, 0, 2, 4)).reshape(capacity, width)
    moment_new, second_new, master_new = adam_rows(
        grad_slots,
        first_moment[0, 0],
        block_second[0, 0],
        master_rows[0, 0],
        assign_here.astype(jnp.float32),
        filled_here,
    )

    low = master_new.astype(jnp.bfloat16).reshape(capacity * CUT, width // CUT)
    low = copies_to_all(copies_to_all(low, "y"), "x").reshape(-1, width // CUT)
    low_other = lax.ppermute(low, "c", SWAP)
    row = jnp.arange(low.shape[0], dtype=jnp.int32)
    from_chip, piece = row // (capacity * CUT), row % (capacity * CUT)
    key_here = (from_chip * nc + core) * capacity * CUT + piece
    key_other = (from_chip * nc + 1 - core) * capacity * CUT + piece
    placed = place_rows(target_here, key_here, low)
    new_weight = place_rows(target_here, key_other, low_other, placed)
    return (new_weight, moment_new[None, None], second_new[None, None], master_new[None, None])


def solution(mesh):
    dp, mp = ("x", "y", "c"), ("zh", "zl")
    fine = Mesh(mesh.devices.reshape(GRID + (-1, PAIR)), dp + mp)
    return jax.shard_map(
        body,
        mesh=fine,
        in_specs=(
            P(dp, mp),
            P(dp, mp),
            P(),
            P(),
            P(mp, dp, None, None),
            P(mp, dp, None),
            P(mp, dp, None, None),
        ),
        out_specs=(
            P(mp, None),
            P(mp, dp, None, None),
            P(mp, dp, None),
            P(mp, dp, None, None),
        ),
        check_vma=False,
    )
```

```python
from functools import partial

import jax
import jax.numpy as jnp
from jax import lax
from jax.experimental import pallas as pl
from jax.experimental.pallas import tpu as pltpu
from jax.sharding import Mesh, PartitionSpec as P

HD = 128
GRID = (4, 8, 2)
PAIR = 2
CUT = 2


beta_one = 0.9
beta_two = 0.95
learn_rate = 0.05
decay_rate = 0.1
epsilon = 1e-08
fix_one = 1.0 - 0.9**10
fix_two = 1.0 - 0.95**10


def block_tables(starts, owners, capacity):
    neuron_ids = jnp.arange(HD, dtype=jnp.int32)
    count_blocks = starts.shape[0]
    block_ids = jnp.sum((starts[None, :] <= neuron_ids[:, None]).astype(jnp.int32), axis=1) - 1
    onehot = block_ids[:, None] == jnp.arange(count_blocks, dtype=jnp.int32)[None, :]
    row_owner = jnp.sum(jnp.where(onehot, owners[None, :], 0), axis=1)
    earlier = (row_owner[:, None] == row_owner[None, :]) & (
        neuron_ids[None, :] < neuron_ids[:, None]
    )
    row_slot = jnp.sum(earlier.astype(jnp.int32), axis=1)
    before_blocks = (owners[:, None] == owners[None, :]) & (starts[None, :] < starts[:, None])
    block_rank = jnp.sum(before_blocks.astype(jnp.int32), axis=1)
    row_rank = jnp.sum(jnp.where(onehot, block_rank[None, :], 0), axis=1)
    return row_owner * capacity + row_slot, row_rank


def adam_rows(grad_slots, moment, second, master, assign, filled):
    width = grad_slots.shape[-1]
    row_squares = jnp.sum(grad_slots * grad_slots, axis=-1)
    block_sums = jnp.sum(assign * row_squares[None, :], axis=-1)
    block_counts = jnp.sum(assign, axis=-1) * width
    block_used = block_counts > 0.0
    block_mean = block_sums / jnp.maximum(block_counts, 1.0)
    second_new = jnp.where(block_used, beta_two * second + (1.0 - beta_two) * block_mean, 0.0)
    slot_second = jnp.sum(assign * second_new[:, None], axis=0)
    slot_second = jnp.where(filled, slot_second, 1.0)
    moment_new = jnp.where(
        filled[..., None], beta_one * moment + (1.0 - beta_one) * grad_slots, 0.0
    )
    update = moment_new / fix_one / (jnp.sqrt(slot_second / fix_two)[..., None] + epsilon)
    master_new = jnp.where(
        filled[..., None], master - learn_rate * (update + decay_rate * master), 0.0
    )
    return (moment_new, second_new, master_new)


SWAP = [(0, 1), (1, 0)]


def copies_to_all(block, axis):
    count = lax.axis_size(axis)
    return lax.all_to_all(jnp.broadcast_to(block[None], (count,) + block.shape), axis, 0, 0, tiled=True)


TOKEN_DOT = (((0,), (0,)), ((), ()))
PARAMS = pltpu.CompilerParams(vmem_limit_bytes=32 * 2**20)


def cost(flops, moved):
    return pl.CostEstimate(flops=flops, bytes_accessed=moved, transcendentals=0)


def first_kernel(cot_ref, own_ref, near_ref, out_ref):
    half = own_ref.shape[1]
    for part, act_ref in enumerate((own_ref, near_ref)):
        out_ref[0, :, part * half : (part + 1) * half] = lax.dot_general(
            cot_ref[0], act_ref[...], TOKEN_DOT, preferred_element_type=jnp.float32
        )


def padded_kernel(target_ref, first_ref, cot_ref, own_ref, near_ref, out_ref):
    chips, cores, _, rows, half = out_ref.shape
    capacity = rows // 2
    row = lax.broadcasted_iota(jnp.int32, (chips * cores * rows, HD), 0)
    slot = row // rows * capacity + row % capacity
    taken = slot == target_ref[0]
    padded = jnp.zeros((chips * cores * rows, half), jnp.float32)
    for part, act_ref in enumerate((own_ref, near_ref)):
        grad = first_ref[0, :, part * half : (part + 1) * half] + lax.dot_general(
            cot_ref[0], act_ref[...], TOKEN_DOT, preferred_element_type=jnp.float32
        )
        high = grad.astype(jnp.bfloat16)
        low = (grad - high.astype(jnp.float32)).astype(jnp.bfloat16)
        pick = jnp.where(taken & (row // capacity % 2 == part), 0.5, 0.0).astype(jnp.bfloat16)
        padded += jnp.dot(
            jnp.concatenate([pick, pick], axis=1),
            jnp.concatenate([high, low], axis=0),
            preferred_element_type=jnp.float32,
        )
    out_ref[:, :, 0] = padded.reshape(chips, cores, rows, half)


def padded_gradient(target, cot_here, cot_other, act_here, act_other, chips, cores, capacity):
    heads, tokens, _ = cot_here.shape
    half = act_here[0].shape[1]
    features = 2 * half
    cot = pl.BlockSpec((1, tokens, HD), lambda h: (h, 0, 0))
    act = pl.BlockSpec((tokens, half), lambda h: (0, 0))
    grad = pl.BlockSpec((1, HD, features), lambda h: (h, 0, 0))
    first = pl.pallas_call(
        first_kernel,
        grid=(heads,),
        in_specs=[cot, act, act],
        out_specs=grad,
        out_shape=jax.ShapeDtypeStruct((heads, HD, features), jnp.float32),
        compiler_params=PARAMS,
        cost_estimate=cost(2 * heads * tokens * HD * features, 2 * 2**20),
    )(cot_here, *act_here)
    tail = (2 * capacity, half)
    return pl.pallas_call(
        padded_kernel,
        grid=(heads,),
        in_specs=[pl.BlockSpec((1, 1, HD), lambda h: (h, 0, 0)), grad, cot, act, act],
        out_specs=pl.BlockSpec((chips, cores, 1) + tail, lambda h: (0, 0, h, 0, 0)),
        out_shape=jax.ShapeDtypeStruct((chips, cores, heads) + tail, jnp.float32),
        compiler_params=PARAMS,
        cost_estimate=cost(4 * heads * tokens * HD * features, 4 * 2**20),
    )(target[:, None, :], first, cot_other, *act_other)


def place_kernel(target_ref, key_ref, rows_ref, *refs):
    want = target_ref[...] * CUT + pl.program_id(0)
    pick = jnp.where(want == key_ref[...], 1.0, 0.0).astype(jnp.bfloat16)
    placed = jnp.dot(pick, rows_ref[...], preferred_element_type=jnp.float32)
    for ref in refs[:-1]:
        placed += ref[...].astype(jnp.float32)
    refs[-1][...] = placed.astype(jnp.bfloat16)


def place_rows(target, key, rows, *placed):
    count, piece = rows.shape
    whole = lambda shape: pl.BlockSpec(shape, lambda j: (0, 0))
    piece_spec = pl.BlockSpec((HD, piece), lambda j: (0, j))
    return pl.pallas_call(
        place_kernel,
        grid=(CUT,),
        in_specs=[whole((HD, 1)), whole((1, count)), whole((count, piece))] + [piece_spec] * len(placed),
        out_specs=piece_spec,
        out_shape=jax.ShapeDtypeStruct((HD, CUT * piece), jnp.bfloat16),
        compiler_params=PARAMS,
        cost_estimate=cost(2 * CUT * HD * count * piece, 2 * 2**20),
    )(target[:, None], key[None, :], rows, *placed)


def body(activations, cotangent, block_start, block_owner, first_moment, block_second, master_rows):
    nx, ny, nc = GRID
    capacity, width = first_moment.shape[2], first_moment.shape[3]
    chips = nx * ny
    core, side, pair = lax.axis_index("c"), lax.axis_index("zl"), lax.axis_index("zh")
    pairs = lax.axis_size("zh")
    chip = lax.axis_index("x") * ny + lax.axis_index("y")
    owner_here = chip * nc + core
    half = activations.shape[1] // 2

    cot_here = copies_to_all(cotangent, "zh")
    keep = lax.dynamic_slice_in_dim(activations, core * half, half, 1)
    give = lax.dynamic_slice_in_dim(activations, (1 - core) * half, half, 1)
    depth = PAIR * pairs
    to_chip = lambda core_to, z: core_to * depth + (z + 2 * core_to - 1) % depth
    same = [(c * depth + z, to_chip(c, z)) for c in range(nc) for z in range(depth)]
    cross = [(c * depth + z, to_chip(1 - c, z)) for c in range(nc) for z in range(depth)]
    act_here = (keep, lax.ppermute(keep, ("c", "zh", "zl"), same))
    act_other = (lax.ppermute(give, "c", SWAP), lax.ppermute(give, ("c", "zh", "zl"), cross))
    cot_other = lax.ppermute(cot_here, "c", SWAP)

    def of_side(table):
        return lax.dynamic_index_in_dim(table.reshape(pairs, PAIR, -1), side, 1, keepdims=False)

    target, row_rank = jax.vmap(partial(block_tables, capacity=capacity))(
        of_side(block_start), of_side(block_owner)
    )
    target_here = lax.dynamic_index_in_dim(target, pair, 0, keepdims=False)
    rank_here = lax.dynamic_index_in_dim(row_rank, pair, 0, keepdims=False)
    slot_ids = owner_here * capacity + jnp.arange(capacity, dtype=jnp.int32)
    mine = slot_ids[:, None] == target_here[None, :]
    filled_here = jnp.any(mine, axis=1)
    slot_rank = jnp.sum(jnp.where(mine, rank_here[None, :], 0), axis=1)
    assign_here = filled_here[None, :] & (
        slot_rank[None, :] == jnp.arange(2, dtype=jnp.int32)[:, None]
    )

    send = padded_gradient(
        target, cot_here, cot_other, act_here, act_other, chips, nc, capacity
    ).astype(jnp.float16)
    send = send.reshape(nx, ny * nc * pairs, 2 * capacity, half)
    got = lax.all_to_all(send, "x", 0, 0, tiled=True)
    send = jnp.sum(got.astype(jnp.float32), axis=0).astype(jnp.float16)
    got = lax.all_to_all(send, ("y", "c", "zh"), 0, 0, tiled=True)
    got = got.reshape(ny, nc, pairs, 2, capacity, half)
    summed = jnp.sum(got.astype(jnp.float32), axis=0) * 2.0
    lower = summed[0].reshape(2 * pairs, capacity, half)
    upper = summed[1, :, ::-1].reshape(2 * pairs, capacity, half)
    lower = jnp.where(side == 0, lower, jnp.roll(lower, 1, 0))
    upper = jnp.where(side == 0, jnp.roll(upper, -1, 0), upper)
    grad_slots = jnp.stack([lower, upper], axis=1)
    grad_slots = jnp.transpose(grad_slots, (2, 0, 1, 3)).reshape(capacity, width)
    moment_new, second_new, master_new = adam_rows(
        grad_slots,
        first_moment[0, 0],
        block_second[0, 0],
        master_rows[0, 0],
        assign_here.astype(jnp.float32),
        filled_here,
    )

    low = master_new.astype(jnp.bfloat16).reshape(capacity * CUT, width // CUT)
    low = copies_to_all(copies_to_all(low, "y"), "x").reshape(-1, width // CUT)
    low_other = lax.ppermute(low, "c", SWAP)
    row = jnp.arange(low.shape[0], dtype=jnp.int32)
    from_chip, piece = row // (capacity * CUT), row % (capacity * CUT)
    key_here = (from_chip * nc + core) * capacity * CUT + piece
    key_other = (from_chip * nc + 1 - core) * capacity * CUT + piece
    placed = place_rows(target_here, key_here, low)
    new_weight = place_rows(target_here, key_other, low_other, placed)
    return (new_weight, moment_new[None, None], second_new[None, None], master_new[None, None])


def solution(mesh):
    dp, mp = ("x", "y", "c"), ("zh", "zl")
    fine = Mesh(mesh.devices.reshape(GRID + (-1, PAIR)), dp + mp)
    return jax.shard_map(
        body,
        mesh=fine,
        in_specs=(
            P(dp, mp),
            P(dp, mp),
            P(),
            P(),
            P(mp, dp, None, None),
            P(mp, dp, None),
            P(mp, dp, None, None),
        ),
        out_specs=(
            P(mp, None),
            P(mp, dp, None, None),
            P(mp, dp, None),
            P(mp, dp, None, None),
        ),
        check_vma=False,
    )
```

```python
from functools import partial

import jax
import jax.numpy as jnp
from jax import lax
from jax.experimental import pallas as pl
from jax.experimental.pallas import tpu as pltpu
from jax.sharding import Mesh, PartitionSpec as P

HD = 128
GRID = (4, 8, 2)
PAIR = 2
CUT = 2


beta_one = 0.9
beta_two = 0.95
learn_rate = 0.05
decay_rate = 0.1
epsilon = 1e-08
fix_one = 1.0 - 0.9**10
fix_two = 1.0 - 0.95**10


def block_tables(starts, owners, capacity):
    neuron_ids = jnp.arange(HD, dtype=jnp.int32)
    count_blocks = starts.shape[0]
    block_ids = jnp.sum((starts[None, :] <= neuron_ids[:, None]).astype(jnp.int32), axis=1) - 1
    onehot = block_ids[:, None] == jnp.arange(count_blocks, dtype=jnp.int32)[None, :]
    row_owner = jnp.sum(jnp.where(onehot, owners[None, :], 0), axis=1)
    earlier = (row_owner[:, None] == row_owner[None, :]) & (
        neuron_ids[None, :] < neuron_ids[:, None]
    )
    row_slot = jnp.sum(earlier.astype(jnp.int32), axis=1)
    before_blocks = (owners[:, None] == owners[None, :]) & (starts[None, :] < starts[:, None])
    block_rank = jnp.sum(before_blocks.astype(jnp.int32), axis=1)
    row_rank = jnp.sum(jnp.where(onehot, block_rank[None, :], 0), axis=1)
    return row_owner * capacity + row_slot, row_rank


def adam_kernel(side_ref, rank_ref, sums_ref, moment_ref, second_ref, master_ref, *outs):
    moment_out, second_out, master_out, rows_out = outs
    even = side_ref[0] == 0
    capacity, width = moment_ref.shape
    half = sums_ref.shape[-1]
    blocks = width // (2 * half)
    low = lambda j: sums_ref[0, j // 2, j % 2]
    high = lambda j: sums_ref[1, j // 2, 1 - j % 2]
    slots = lax.broadcasted_iota(jnp.int32, (capacity, 1), 0)
    rank = sum(jnp.where(slots == slot, rank_ref[slot], 0) for slot in range(capacity))
    grads = []
    for block in range(blocks):
        grads.append(jnp.where(even, low(block), low((block - 1) % blocks)))
        grads.append(jnp.where(even, high((block + 1) % blocks), high(block)))
    squares = sum(jnp.sum(grad * grad, axis=1, keepdims=True) for grad in grads)
    slot_second = jnp.ones((capacity, 1), jnp.float32)
    for slot in range(2):
        here = rank == slot
        count = jnp.sum(jnp.where(here, float(width), 0.0), axis=0, keepdims=True)
        mean = jnp.sum(jnp.where(here, squares, 0.0), axis=0, keepdims=True) / jnp.maximum(count, 1.0)
        fresh = beta_two * second_ref[:, slot : slot + 1] + (1.0 - beta_two) * mean
        fresh = jnp.where(count > 0.0, fresh, 0.0)
        second_out[:, slot : slot + 1] = fresh
        slot_second = jnp.where(here, fresh, slot_second)
    filled = rank >= 0
    scale = 1.0 / (fix_one * (jnp.sqrt(slot_second / fix_two) + epsilon))
    for part, grad in enumerate(grads):
        span = slice(part * half, (part + 1) * half)
        moment = jnp.where(filled, beta_one * moment_ref[:, span] + (1.0 - beta_one) * grad, 0.0)
        master = master_ref[:, span]
        master = master - learn_rate * (moment * scale + decay_rate * master)
        master = jnp.where(filled, master, 0.0)
        moment_out[:, span] = moment
        master_out[:, span] = master
        piece, place = divmod(part * half, width // CUT)
        rows_out[piece * capacity : (piece + 1) * capacity, place : place + half] = master


def adam_rows(side, rank, sums, moment, second, master):
    capacity, width = moment.shape
    shape = lambda *dims: jax.ShapeDtypeStruct(dims, jnp.float32)
    vmem = pl.BlockSpec(memory_space=pltpu.VMEM)
    return pl.pallas_call(
        adam_kernel,
        in_specs=[pl.BlockSpec(memory_space=pltpu.SMEM)] * 2 + [vmem] * 4,
        out_specs=[vmem] * 4,
        out_shape=[
            shape(capacity, width),
            shape(1, 2),
            shape(capacity, width),
            shape(capacity * CUT, width // CUT),
        ],
        compiler_params=pltpu.CompilerParams(vmem_limit_bytes=32 * 2**20),
    )(side[None], rank, sums, moment, second[None], master)


SWAP = [(0, 1), (1, 0)]


def copies_to_all(block, axis):
    count = lax.axis_size(axis)
    return lax.all_to_all(jnp.broadcast_to(block[None], (count,) + block.shape), axis, 0, 0, tiled=True)


TOKEN_DOT = (((0,), (0,)), ((), ()))
PARAMS = pltpu.CompilerParams(vmem_limit_bytes=32 * 2**20)


def cost(flops, moved):
    return pl.CostEstimate(flops=flops, bytes_accessed=moved, transcendentals=0)


def first_kernel(cot_ref, own_ref, near_ref, out_ref):
    half = own_ref.shape[1]
    for part, act_ref in enumerate((own_ref, near_ref)):
        out_ref[0, :, part * half : (part + 1) * half] = lax.dot_general(
            cot_ref[0], act_ref[...], TOKEN_DOT, preferred_element_type=jnp.float32
        )


def padded_kernel(target_ref, first_ref, cot_ref, own_ref, near_ref, out_ref):
    chips, cores, _, rows, half = out_ref.shape
    capacity = rows // 2
    row = lax.broadcasted_iota(jnp.int32, (chips * cores * rows, HD), 0)
    slot = row // rows * capacity + row % capacity
    taken = slot == target_ref[0]
    padded = jnp.zeros((chips * cores * rows, half), jnp.float32)
    for part, act_ref in enumerate((own_ref, near_ref)):
        grad = first_ref[0, :, part * half : (part + 1) * half] + lax.dot_general(
            cot_ref[0], act_ref[...], TOKEN_DOT, preferred_element_type=jnp.float32
        )
        high = grad.astype(jnp.bfloat16)
        low = (grad - high.astype(jnp.float32)).astype(jnp.bfloat16)
        pick = jnp.where(taken & (row // capacity % 2 == part), 0.5, 0.0).astype(jnp.bfloat16)
        padded += jnp.dot(
            jnp.concatenate([pick, pick], axis=1),
            jnp.concatenate([high, low], axis=0),
            preferred_element_type=jnp.float32,
        )
    out_ref[:, :, 0] = padded.reshape(chips, cores, rows, half)


def padded_gradient(target, cot_here, cot_other, act_here, act_other, chips, cores, capacity):
    heads, tokens, _ = cot_here.shape
    half = act_here[0].shape[1]
    features = 2 * half
    cot = pl.BlockSpec((1, tokens, HD), lambda h: (h, 0, 0))
    act = pl.BlockSpec((tokens, half), lambda h: (0, 0))
    grad = pl.BlockSpec((1, HD, features), lambda h: (h, 0, 0))
    first = pl.pallas_call(
        first_kernel,
        grid=(heads,),
        in_specs=[cot, act, act],
        out_specs=grad,
        out_shape=jax.ShapeDtypeStruct((heads, HD, features), jnp.float32),
        compiler_params=PARAMS,
        cost_estimate=cost(2 * heads * tokens * HD * features, 2 * 2**20),
    )(cot_here, *act_here)
    tail = (2 * capacity, half)
    return pl.pallas_call(
        padded_kernel,
        grid=(heads,),
        in_specs=[pl.BlockSpec((1, 1, HD), lambda h: (h, 0, 0)), grad, cot, act, act],
        out_specs=pl.BlockSpec((chips, cores, 1) + tail, lambda h: (0, 0, h, 0, 0)),
        out_shape=jax.ShapeDtypeStruct((chips, cores, heads) + tail, jnp.float32),
        compiler_params=PARAMS,
        cost_estimate=cost(4 * heads * tokens * HD * features, 4 * 2**20),
    )(target[:, None, :], first, cot_other, *act_other)


def place_kernel(target_ref, key_ref, rows_ref, *refs):
    want = target_ref[...] * CUT + pl.program_id(0)
    pick = jnp.where(want == key_ref[...], 1.0, 0.0).astype(jnp.bfloat16)
    placed = jnp.dot(pick, rows_ref[...], preferred_element_type=jnp.float32)
    for ref in refs[:-1]:
        placed += ref[...].astype(jnp.float32)
    refs[-1][...] = placed.astype(jnp.bfloat16)


def place_rows(target, key, rows, *placed):
    count, piece = rows.shape
    whole = lambda shape: pl.BlockSpec(shape, lambda j: (0, 0))
    piece_spec = pl.BlockSpec((HD, piece), lambda j: (0, j))
    return pl.pallas_call(
        place_kernel,
        grid=(CUT,),
        in_specs=[whole((HD, 1)), whole((1, count)), whole((count, piece))] + [piece_spec] * len(placed),
        out_specs=piece_spec,
        out_shape=jax.ShapeDtypeStruct((HD, CUT * piece), jnp.bfloat16),
        compiler_params=PARAMS,
        cost_estimate=cost(2 * CUT * HD * count * piece, 2 * 2**20),
    )(target, key, rows, *placed)


def body(activations, cotangent, block_start, block_owner, first_moment, block_second, master_rows):
    nx, ny, nc = GRID
    capacity, width = first_moment.shape[2], first_moment.shape[3]
    chips = nx * ny
    core, side, pair = lax.axis_index("c"), lax.axis_index("zl"), lax.axis_index("zh")
    pairs = lax.axis_size("zh")
    chip = lax.axis_index("x") * ny + lax.axis_index("y")
    owner_here = chip * nc + core
    half = activations.shape[1] // 2

    cot_here = copies_to_all(cotangent, "zh")
    def of_side(table):
        return lax.dynamic_index_in_dim(table.reshape(pairs, PAIR, -1), side, 1, keepdims=False)

    target, row_rank = jax.vmap(partial(block_tables, capacity=capacity))(
        of_side(block_start), of_side(block_owner)
    )
    target, activations = lax.optimization_barrier((target, activations))
    keep = lax.dynamic_slice_in_dim(activations, core * half, half, 1)
    give = lax.dynamic_slice_in_dim(activations, (1 - core) * half, half, 1)
    depth = PAIR * pairs
    to_chip = lambda core_to, z: core_to * depth + (z + 2 * core_to - 1) % depth
    same = [(c * depth + z, to_chip(c, z)) for c in range(nc) for z in range(depth)]
    cross = [(c * depth + z, to_chip(1 - c, z)) for c in range(nc) for z in range(depth)]
    act_here = (keep, lax.ppermute(keep, ("c", "zh", "zl"), same))
    act_other = (lax.ppermute(give, "c", SWAP), lax.ppermute(give, ("c", "zh", "zl"), cross))
    cot_other = lax.ppermute(cot_here, "c", SWAP)

    target_here = lax.dynamic_index_in_dim(target, pair, 0, keepdims=False)
    rank_here = lax.dynamic_index_in_dim(row_rank, pair, 0, keepdims=False)
    slot_ids = owner_here * capacity + jnp.arange(capacity, dtype=jnp.int32)
    mine = slot_ids[:, None] == target_here[None, :]
    rank = jnp.max(jnp.where(mine, rank_here[None, :], -1), axis=1)
    row = jnp.arange(chips * capacity * CUT, dtype=jnp.int32)
    from_chip, cut, slot = row // (capacity * CUT), row // capacity % CUT, row % capacity
    key_here = ((from_chip * nc + core) * capacity + slot) * CUT + cut
    key_other = ((from_chip * nc + 1 - core) * capacity + slot) * CUT + cut

    send = padded_gradient(
        target, cot_here, cot_other, act_here, act_other, chips, nc, capacity
    ).astype(jnp.float16)
    send = send.reshape(nx, ny * nc * pairs, 2 * capacity, half)
    send, target_here, rank, key_here, key_other = lax.optimization_barrier(
        (send, target_here[:, None], rank, key_here[None, :], key_other[None, :])
    )
    got = lax.all_to_all(send, "x", 0, 0, tiled=True)
    send = jnp.sum(got.astype(jnp.float32), axis=0).astype(jnp.float16)
    got = lax.all_to_all(send, ("y", "c", "zh"), 0, 0, tiled=True)
    got = got.reshape(ny, nc, pairs, 2, capacity, half)
    summed = jnp.sum(got.astype(jnp.float32), axis=0) * 2.0
    moment_new, second_new, master_new, low = adam_rows(
        side, rank, summed, first_moment[0, 0], block_second[0, 0], master_rows[0, 0]
    )

    low = copies_to_all(copies_to_all(low.astype(jnp.bfloat16), "y"), "x")
    low = low.reshape(-1, width // CUT)
    low_other = lax.ppermute(low, "c", SWAP)
    placed = place_rows(target_here, key_here, low)
    new_weight = place_rows(target_here, key_other, low_other, placed)
    return (new_weight, moment_new[None, None], second_new[None], master_new[None, None])


def solution(mesh):
    dp, mp = ("x", "y", "c"), ("zh", "zl")
    fine = Mesh(mesh.devices.reshape(GRID + (-1, PAIR)), dp + mp)
    return jax.shard_map(
        body,
        mesh=fine,
        in_specs=(
            P(dp, mp),
            P(dp, mp),
            P(),
            P(),
            P(mp, dp, None, None),
            P(mp, dp, None),
            P(mp, dp, None, None),
        ),
        out_specs=(
            P(mp, None),
            P(mp, dp, None, None),
            P(mp, dp, None),
            P(mp, dp, None, None),
        ),
        check_vma=False,
    )
```

```python
from functools import partial

import jax
import jax.numpy as jnp
from jax import lax
from jax.experimental import pallas as pl
from jax.experimental.pallas import tpu as pltpu
from jax.sharding import Mesh, PartitionSpec as P

HD = 128
GRID = (4, 8, 2)
PAIR = 2
CUT = 2


beta_one = 0.9
beta_two = 0.95
learn_rate = 0.05
decay_rate = 0.1
epsilon = 1e-08
fix_one = 1.0 - 0.9**10
fix_two = 1.0 - 0.95**10


def block_tables(starts, owners, capacity):
    neuron_ids = jnp.arange(HD, dtype=jnp.int32)
    count_blocks = starts.shape[0]
    block_ids = jnp.sum((starts[None, :] <= neuron_ids[:, None]).astype(jnp.int32), axis=1) - 1
    onehot = block_ids[:, None] == jnp.arange(count_blocks, dtype=jnp.int32)[None, :]
    row_owner = jnp.sum(jnp.where(onehot, owners[None, :], 0), axis=1)
    earlier = (row_owner[:, None] == row_owner[None, :]) & (
        neuron_ids[None, :] < neuron_ids[:, None]
    )
    row_slot = jnp.sum(earlier.astype(jnp.int32), axis=1)
    before_blocks = (owners[:, None] == owners[None, :]) & (starts[None, :] < starts[:, None])
    block_rank = jnp.sum(before_blocks.astype(jnp.int32), axis=1)
    row_rank = jnp.sum(jnp.where(onehot, block_rank[None, :], 0), axis=1)
    return row_owner * capacity + row_slot, row_rank


def adam_kernel(side_ref, rank_ref, sums_ref, moment_ref, second_ref, master_ref, *outs):
    moment_out, second_out, master_out, rows_out = outs
    even = side_ref[0] == 0
    capacity, width = moment_ref.shape
    half = sums_ref.shape[-1]
    blocks = width // (2 * half)
    low = lambda j: sums_ref[j // 2, 0, j % 2]
    high = lambda j: sums_ref[j // 2, 1, 1 - j % 2]
    slots = lax.broadcasted_iota(jnp.int32, (capacity, 1), 0)
    rank = sum(jnp.where(slots == slot, rank_ref[slot], 0) for slot in range(capacity))
    grads = []
    for block in range(blocks):
        grads.append(jnp.where(even, low(block), low((block - 1) % blocks)))
        grads.append(jnp.where(even, high((block + 1) % blocks), high(block)))
    squares = sum(jnp.sum(grad * grad, axis=1, keepdims=True) for grad in grads)
    slot_second = jnp.ones((capacity, 1), jnp.float32)
    for slot in range(2):
        here = rank == slot
        count = jnp.sum(jnp.where(here, float(width), 0.0), axis=0, keepdims=True)
        mean = jnp.sum(jnp.where(here, squares, 0.0), axis=0, keepdims=True) / jnp.maximum(count, 1.0)
        fresh = beta_two * second_ref[:, slot : slot + 1] + (1.0 - beta_two) * mean
        fresh = jnp.where(count > 0.0, fresh, 0.0)
        second_out[:, slot : slot + 1] = fresh
        slot_second = jnp.where(here, fresh, slot_second)
    filled = rank >= 0
    scale = 1.0 / (fix_one * (jnp.sqrt(slot_second / fix_two) + epsilon))
    for part, grad in enumerate(grads):
        span = slice(part * half, (part + 1) * half)
        moment = jnp.where(filled, beta_one * moment_ref[:, span] + (1.0 - beta_one) * grad, 0.0)
        master = master_ref[:, span]
        master = master - learn_rate * (moment * scale + decay_rate * master)
        master = jnp.where(filled, master, 0.0)
        moment_out[:, span] = moment
        master_out[:, span] = master
        piece, place = divmod(part * half, width // CUT)
        rows_out[piece * capacity : (piece + 1) * capacity, place : place + half] = master


def adam_rows(side, rank, sums, moment, second, master):
    capacity, width = moment.shape
    shape = lambda *dims: jax.ShapeDtypeStruct(dims, jnp.float32)
    vmem = pl.BlockSpec(memory_space=pltpu.VMEM)
    return pl.pallas_call(
        adam_kernel,
        in_specs=[pl.BlockSpec(memory_space=pltpu.SMEM)] * 2 + [vmem] * 4,
        out_specs=[vmem] * 4,
        out_shape=[
            shape(capacity, width),
            shape(1, 2),
            shape(capacity, width),
            shape(capacity * CUT, width // CUT),
        ],
        compiler_params=pltpu.CompilerParams(vmem_limit_bytes=32 * 2**20),
    )(side[None], rank, sums, moment, second[None], master)


SWAP = [(0, 1), (1, 0)]


def copies_to_all(block, axis):
    count = lax.axis_size(axis)
    return lax.all_to_all(jnp.broadcast_to(block[None], (count,) + block.shape), axis, 0, 0, tiled=True)


TOKEN_DOT = (((0,), (0,)), ((), ()))
PARAMS = pltpu.CompilerParams(vmem_limit_bytes=32 * 2**20)


def cost(flops, moved):
    return pl.CostEstimate(flops=flops, bytes_accessed=moved, transcendentals=0)


def first_kernel(cot_ref, own_ref, near_ref, out_ref):
    half = own_ref.shape[1]
    for part, act_ref in enumerate((own_ref, near_ref)):
        out_ref[0, :, part * half : (part + 1) * half] = lax.dot_general(
            cot_ref[0], act_ref[...], TOKEN_DOT, preferred_element_type=jnp.float32
        )


def padded_kernel(target_ref, first_ref, cot_ref, own_ref, near_ref, out_ref):
    lines, spots, _, rows, half = out_ref.shape
    count, cores, capacity = lines * spots * rows, GRID[2], rows // 2
    row = lax.broadcasted_iota(jnp.int32, (count, HD), 0)
    line, spot = row // (spots * rows), row // rows % spots
    owner = (line // cores * spots + spot) * cores + line % cores
    taken = owner * capacity + row % capacity == target_ref[0]
    padded = jnp.zeros((count, half), jnp.float32)
    for part, act_ref in enumerate((own_ref, near_ref)):
        grad = first_ref[0, :, part * half : (part + 1) * half] + lax.dot_general(
            cot_ref[0], act_ref[...], TOKEN_DOT, preferred_element_type=jnp.float32
        )
        high = grad.astype(jnp.bfloat16)
        low = (grad - high.astype(jnp.float32)).astype(jnp.bfloat16)
        pick = jnp.where(taken & (row // capacity % 2 == part), 0.5, 0.0).astype(jnp.bfloat16)
        padded += jnp.dot(
            jnp.concatenate([pick, pick], axis=1),
            jnp.concatenate([high, low], axis=0),
            preferred_element_type=jnp.float32,
        )
    out_ref[:, :, 0] = padded.reshape(lines, spots, rows, half)


def padded_gradient(target, cot_here, cot_other, act_here, act_other, lines, spots, capacity):
    heads, tokens, _ = cot_here.shape
    half = act_here[0].shape[1]
    features = 2 * half
    cot = pl.BlockSpec((1, tokens, HD), lambda h: (h, 0, 0))
    act = pl.BlockSpec((tokens, half), lambda h: (0, 0))
    grad = pl.BlockSpec((1, HD, features), lambda h: (h, 0, 0))
    first = pl.pallas_call(
        first_kernel,
        grid=(heads,),
        in_specs=[cot, act, act],
        out_specs=grad,
        out_shape=jax.ShapeDtypeStruct((heads, HD, features), jnp.float32),
        compiler_params=PARAMS,
        cost_estimate=cost(2 * heads * tokens * HD * features, 2 * 2**20),
    )(cot_here, *act_here)
    tail = (2 * capacity, half)
    return pl.pallas_call(
        padded_kernel,
        grid=(heads,),
        in_specs=[pl.BlockSpec((1, 1, HD), lambda h: (h, 0, 0)), grad, cot, act, act],
        out_specs=pl.BlockSpec((lines, spots, 1) + tail, lambda h: (0, 0, h, 0, 0)),
        out_shape=jax.ShapeDtypeStruct((lines, spots, heads) + tail, jnp.float32),
        compiler_params=PARAMS,
        cost_estimate=cost(4 * heads * tokens * HD * features, 4 * 2**20),
    )(target[:, None, :], first, cot_other, *act_other)


def place_kernel(target_ref, key_ref, rows_ref, *refs):
    want = target_ref[...] * CUT + pl.program_id(0)
    pick = jnp.where(want == key_ref[...], 1.0, 0.0).astype(jnp.bfloat16)
    placed = jnp.dot(pick, rows_ref[...], preferred_element_type=jnp.float32)
    for ref in refs[:-1]:
        placed += ref[...].astype(jnp.float32)
    refs[-1][...] = placed.astype(jnp.bfloat16)


def place_rows(target, key, rows, *placed):
    count, piece = rows.shape
    whole = lambda shape: pl.BlockSpec(shape, lambda j: (0, 0))
    piece_spec = pl.BlockSpec((HD, piece), lambda j: (0, j))
    return pl.pallas_call(
        place_kernel,
        grid=(CUT,),
        in_specs=[whole((HD, 1)), whole((1, count)), whole((count, piece))] + [piece_spec] * len(placed),
        out_specs=piece_spec,
        out_shape=jax.ShapeDtypeStruct((HD, CUT * piece), jnp.bfloat16),
        compiler_params=PARAMS,
        cost_estimate=cost(2 * CUT * HD * count * piece, 2 * 2**20),
    )(target, key, rows, *placed)


def body(activations, cotangent, block_start, block_owner, first_moment, block_second, master_rows):
    nx, ny, nc = GRID
    capacity, width = first_moment.shape[2], first_moment.shape[3]
    chips = nx * ny
    core, side, pair = lax.axis_index("c"), lax.axis_index("zl"), lax.axis_index("zh")
    pairs = lax.axis_size("zh")
    chip = lax.axis_index("x") * ny + lax.axis_index("y")
    owner_here = chip * nc + core
    half = activations.shape[1] // 2

    cot_here = copies_to_all(cotangent, "zh")
    def of_side(table):
        return lax.dynamic_index_in_dim(table.reshape(pairs, PAIR, -1), side, 1, keepdims=False)

    target, row_rank = jax.vmap(partial(block_tables, capacity=capacity))(
        of_side(block_start), of_side(block_owner)
    )
    target, activations = lax.optimization_barrier((target, activations))
    keep = lax.dynamic_slice_in_dim(activations, core * half, half, 1)
    give = lax.dynamic_slice_in_dim(activations, (1 - core) * half, half, 1)
    depth = PAIR * pairs
    to_chip = lambda core_to, z: core_to * depth + (z + 2 * core_to - 1) % depth
    same = [(c * depth + z, to_chip(c, z)) for c in range(nc) for z in range(depth)]
    cross = [(c * depth + z, to_chip(1 - c, z)) for c in range(nc) for z in range(depth)]
    act_here = (keep, lax.ppermute(keep, ("c", "zh", "zl"), same))
    act_other = (lax.ppermute(give, "c", SWAP), lax.ppermute(give, ("c", "zh", "zl"), cross))
    cot_other = lax.ppermute(cot_here, "c", SWAP)

    target_here = lax.dynamic_index_in_dim(target, pair, 0, keepdims=False)
    rank_here = lax.dynamic_index_in_dim(row_rank, pair, 0, keepdims=False)
    slot_ids = owner_here * capacity + jnp.arange(capacity, dtype=jnp.int32)
    mine = slot_ids[:, None] == target_here[None, :]
    rank = jnp.max(jnp.where(mine, rank_here[None, :], -1), axis=1)
    row = jnp.arange(chips * capacity * CUT, dtype=jnp.int32)
    from_chip, cut, slot = row // (capacity * CUT), row // capacity % CUT, row % capacity
    key_here = ((from_chip * nc + core) * capacity + slot) * CUT + cut
    key_other = ((from_chip * nc + 1 - core) * capacity + slot) * CUT + cut

    send = padded_gradient(
        target, cot_here, cot_other, act_here, act_other, nx * nc, ny, capacity
    ).astype(jnp.float16)
    send = send.reshape(nx * nc, ny * pairs, 2 * capacity, half)
    send, target_here, rank, key_here, key_other = lax.optimization_barrier(
        (send, target_here[:, None], rank, key_here[None, :], key_other[None, :])
    )
    got = lax.all_to_all(send, ("x", "c"), 0, 0, tiled=True)
    got = got.reshape(nx, nc, ny * pairs, 2 * capacity, half)
    send = jnp.sum(got.astype(jnp.float32), axis=0).astype(jnp.float16)
    got = lax.all_to_all(jnp.swapaxes(send, 0, 1), ("y", "zh"), 0, 0, tiled=True)
    got = got.reshape(ny, pairs, nc, 2, capacity, half)
    summed = jnp.sum(got.astype(jnp.float32), axis=0) * 2.0
    moment_new, second_new, master_new, low = adam_rows(
        side, rank, summed, first_moment[0, 0], block_second[0, 0], master_rows[0, 0]
    )

    low = copies_to_all(copies_to_all(low.astype(jnp.bfloat16), "y"), "x")
    low = low.reshape(-1, width // CUT)
    low_other = lax.ppermute(low, "c", SWAP)
    placed = place_rows(target_here, key_here, low)
    new_weight = place_rows(target_here, key_other, low_other, placed)
    return (new_weight, moment_new[None, None], second_new[None], master_new[None, None])


def solution(mesh):
    dp, mp = ("x", "y", "c"), ("zh", "zl")
    fine = Mesh(mesh.devices.reshape(GRID + (-1, PAIR)), dp + mp)
    return jax.shard_map(
        body,
        mesh=fine,
        in_specs=(
            P(dp, mp),
            P(dp, mp),
            P(),
            P(),
            P(mp, dp, None, None),
            P(mp, dp, None),
            P(mp, dp, None, None),
        ),
        out_specs=(
            P(mp, None),
            P(mp, dp, None, None),
            P(mp, dp, None),
            P(mp, dp, None, None),
        ),
        check_vma=False,
    )
```

```python
from functools import partial

import jax
import jax.numpy as jnp
from jax import lax
from jax.experimental import pallas as pl
from jax.experimental.pallas import tpu as pltpu
from jax.sharding import Mesh, PartitionSpec as P

HD = 128
GRID = (4, 8, 2)
PAIR = 2
CUT = 2


beta_one = 0.9
beta_two = 0.95
learn_rate = 0.05
decay_rate = 0.1
epsilon = 1e-08
fix_one = 1.0 - 0.9**10
fix_two = 1.0 - 0.95**10


def block_tables(starts, owners, capacity):
    neuron_ids = jnp.arange(HD, dtype=jnp.int32)
    count_blocks = starts.shape[0]
    block_ids = jnp.sum((starts[None, :] <= neuron_ids[:, None]).astype(jnp.int32), axis=1) - 1
    onehot = block_ids[:, None] == jnp.arange(count_blocks, dtype=jnp.int32)[None, :]
    row_owner = jnp.sum(jnp.where(onehot, owners[None, :], 0), axis=1)
    earlier = (row_owner[:, None] == row_owner[None, :]) & (
        neuron_ids[None, :] < neuron_ids[:, None]
    )
    row_slot = jnp.sum(earlier.astype(jnp.int32), axis=1)
    before_blocks = (owners[:, None] == owners[None, :]) & (starts[None, :] < starts[:, None])
    block_rank = jnp.sum(before_blocks.astype(jnp.int32), axis=1)
    row_rank = jnp.sum(jnp.where(onehot, block_rank[None, :], 0), axis=1)
    return row_owner * capacity + row_slot, row_rank


def adam_kernel(side_ref, rank_ref, sums_ref, moment_ref, second_ref, master_ref, *outs):
    moment_out, second_out, master_out, rows_out = outs
    even = side_ref[0] == 0
    capacity, width = moment_ref.shape
    half = sums_ref.shape[-1]
    blocks = width // (2 * half)
    low = lambda j: sums_ref[j // 2, 0, j % 2]
    high = lambda j: sums_ref[j // 2, 1, 1 - j % 2]
    slots = lax.broadcasted_iota(jnp.int32, (capacity, 1), 0)
    rank = sum(jnp.where(slots == slot, rank_ref[slot], 0) for slot in range(capacity))
    grads = []
    for block in range(blocks):
        grads.append(jnp.where(even, low(block), low((block - 1) % blocks)))
        grads.append(jnp.where(even, high((block + 1) % blocks), high(block)))
    squares = sum(jnp.sum(grad * grad, axis=1, keepdims=True) for grad in grads)
    slot_second = jnp.ones((capacity, 1), jnp.float32)
    for slot in range(2):
        here = rank == slot
        count = jnp.sum(jnp.where(here, float(width), 0.0), axis=0, keepdims=True)
        mean = jnp.sum(jnp.where(here, squares, 0.0), axis=0, keepdims=True) / jnp.maximum(count, 1.0)
        fresh = beta_two * second_ref[:, slot : slot + 1] + (1.0 - beta_two) * mean
        fresh = jnp.where(count > 0.0, fresh, 0.0)
        second_out[:, slot : slot + 1] = fresh
        slot_second = jnp.where(here, fresh, slot_second)
    filled = rank >= 0
    scale = 1.0 / (fix_one * (jnp.sqrt(slot_second / fix_two) + epsilon))
    for part, grad in enumerate(grads):
        span = slice(part * half, (part + 1) * half)
        moment = jnp.where(filled, beta_one * moment_ref[:, span] + (1.0 - beta_one) * grad, 0.0)
        master = master_ref[:, span]
        master = master - learn_rate * (moment * scale + decay_rate * master)
        master = jnp.where(filled, master, 0.0)
        moment_out[:, span] = moment
        master_out[:, span] = master
        piece, place = divmod(part * half, width // CUT)
        rows_out[piece * capacity : (piece + 1) * capacity, place : place + half] = master


def adam_rows(side, rank, sums, moment, second, master):
    capacity, width = moment.shape
    shape = lambda *dims: jax.ShapeDtypeStruct(dims, jnp.float32)
    vmem = pl.BlockSpec(memory_space=pltpu.VMEM)
    return pl.pallas_call(
        adam_kernel,
        in_specs=[pl.BlockSpec(memory_space=pltpu.SMEM)] * 2 + [vmem] * 4,
        out_specs=[vmem] * 4,
        out_shape=[
            shape(capacity, width),
            shape(1, 2),
            shape(capacity, width),
            shape(capacity * CUT, width // CUT),
        ],
        compiler_params=pltpu.CompilerParams(vmem_limit_bytes=32 * 2**20),
    )(side[None], rank, sums, moment, second[None], master)


SWAP = [(0, 1), (1, 0)]


def copies_to_all(block, axis):
    count = lax.axis_size(axis)
    return lax.all_to_all(jnp.broadcast_to(block[None], (count,) + block.shape), axis, 0, 0, tiled=True)


TOKEN_DOT = (((0,), (0,)), ((), ()))
PARAMS = pltpu.CompilerParams(vmem_limit_bytes=32 * 2**20)


def cost(flops, moved):
    return pl.CostEstimate(flops=flops, bytes_accessed=moved, transcendentals=0)


def first_kernel(cot_ref, act_ref, out_ref):
    for head in range(cot_ref.shape[0]):
        out_ref[head] = lax.dot_general(
            cot_ref[head], act_ref[...], TOKEN_DOT, preferred_element_type=jnp.float32
        )


def padded_kernel(target_ref, first_ref, here_ref, other_ref, own_ref, near_ref, far_ref, out_ref):
    lines, spots, heads, rows, half = out_ref.shape
    count, cores, capacity = lines * spots * rows, GRID[2], rows // 2
    row = lax.broadcasted_iota(jnp.int32, (count, HD), 0)
    line, spot = row // (spots * rows), row // rows % spots
    owner = (line // cores * spots + spot) * cores + line % cores
    slot, part_of = owner * capacity + row % capacity, row // capacity % 2
    dot = partial(lax.dot_general, dimension_numbers=TOKEN_DOT, preferred_element_type=jnp.float32)
    for head in range(heads):
        taken = slot == target_ref[head]
        own = first_ref[head] + dot(other_ref[head], own_ref[...])
        near = dot(here_ref[head], near_ref[...]) + dot(other_ref[head], far_ref[...])
        padded = jnp.zeros((count, half), jnp.float32)
        for part, grad in enumerate((own, near)):
            high = grad.astype(jnp.bfloat16)
            low = (grad - high.astype(jnp.float32)).astype(jnp.bfloat16)
            pick = jnp.where(taken & (part_of == part), 0.5, 0.0).astype(jnp.bfloat16)
            padded += jnp.dot(
                jnp.concatenate([pick, pick], axis=1),
                jnp.concatenate([high, low], axis=0),
                preferred_element_type=jnp.float32,
            )
        out_ref[:, :, head] = padded.reshape(lines, spots, rows, half)


def padded_gradient(target, cot_here, cot_other, act_here, act_other, lines, spots, capacity):
    heads, tokens, _ = cot_here.shape
    half = act_here[0].shape[1]
    vmem = pl.BlockSpec(memory_space=pltpu.VMEM)
    first = pl.pallas_call(
        first_kernel,
        in_specs=[vmem] * 2,
        out_specs=vmem,
        out_shape=jax.ShapeDtypeStruct((heads, HD, half), jnp.float32),
        compiler_params=PARAMS,
        cost_estimate=cost(2 * heads * tokens * HD * half, 2**20),
    )(cot_here, act_here[0])
    return pl.pallas_call(
        padded_kernel,
        in_specs=[vmem] * 7,
        out_specs=vmem,
        out_shape=jax.ShapeDtypeStruct((lines, spots, heads, 2 * capacity, half), jnp.float32),
        compiler_params=PARAMS,
        cost_estimate=cost(10 * heads * tokens * HD * half, 4 * 2**20),
    )(target[:, None, :], first, cot_here, cot_other, act_other[0], act_here[1], act_other[1])


def place_kernel(target_ref, key_ref, rows_ref, *refs):
    want = target_ref[...] * CUT + pl.program_id(0)
    pick = jnp.where(want == key_ref[...], 1.0, 0.0).astype(jnp.bfloat16)
    placed = jnp.dot(pick, rows_ref[...], preferred_element_type=jnp.float32)
    for ref in refs[:-1]:
        placed += ref[...].astype(jnp.float32)
    refs[-1][...] = placed.astype(jnp.bfloat16)


def place_rows(target, key, rows, *placed):
    count, piece = rows.shape
    whole = lambda shape: pl.BlockSpec(shape, lambda j: (0, 0))
    piece_spec = pl.BlockSpec((HD, piece), lambda j: (0, j))
    return pl.pallas_call(
        place_kernel,
        grid=(CUT,),
        in_specs=[whole((HD, 1)), whole((1, count)), whole((count, piece))] + [piece_spec] * len(placed),
        out_specs=piece_spec,
        out_shape=jax.ShapeDtypeStruct((HD, CUT * piece), jnp.bfloat16),
        compiler_params=PARAMS,
        cost_estimate=cost(2 * CUT * HD * count * piece, 2 * 2**20),
    )(target, key, rows, *placed)


def body(activations, cotangent, block_start, block_owner, first_moment, block_second, master_rows):
    nx, ny, nc = GRID
    capacity, width = first_moment.shape[2], first_moment.shape[3]
    chips = nx * ny
    core, side, pair = lax.axis_index("c"), lax.axis_index("zl"), lax.axis_index("zh")
    pairs = lax.axis_size("zh")
    chip = lax.axis_index("x") * ny + lax.axis_index("y")
    owner_here = chip * nc + core
    half = activations.shape[1] // 2

    cot_here = copies_to_all(cotangent, "zh")
    def of_side(table):
        return lax.dynamic_index_in_dim(table.reshape(pairs, PAIR, -1), side, 1, keepdims=False)

    target, row_rank = jax.vmap(partial(block_tables, capacity=capacity))(
        of_side(block_start), of_side(block_owner)
    )
    target, activations = lax.optimization_barrier((target, activations))
    keep = lax.dynamic_slice_in_dim(activations, core * half, half, 1)
    give = lax.dynamic_slice_in_dim(activations, (1 - core) * half, half, 1)
    depth = PAIR * pairs
    to_chip = lambda core_to, z: core_to * depth + (z + 2 * core_to - 1) % depth
    same = [(c * depth + z, to_chip(c, z)) for c in range(nc) for z in range(depth)]
    cross = [(c * depth + z, to_chip(1 - c, z)) for c in range(nc) for z in range(depth)]
    act_here = (keep, lax.ppermute(keep, ("c", "zh", "zl"), same))
    act_other = (lax.ppermute(give, "c", SWAP), lax.ppermute(give, ("c", "zh", "zl"), cross))
    cot_other = lax.ppermute(cot_here, "c", SWAP)

    target_here = lax.dynamic_index_in_dim(target, pair, 0, keepdims=False)
    rank_here = lax.dynamic_index_in_dim(row_rank, pair, 0, keepdims=False)
    slot_ids = owner_here * capacity + jnp.arange(capacity, dtype=jnp.int32)
    mine = slot_ids[:, None] == target_here[None, :]
    rank = jnp.max(jnp.where(mine, rank_here[None, :], -1), axis=1)
    row = jnp.arange(chips * capacity * CUT, dtype=jnp.int32)
    from_chip, cut, slot = row // (capacity * CUT), row // capacity % CUT, row % capacity
    key_here = ((from_chip * nc + core) * capacity + slot) * CUT + cut
    key_other = ((from_chip * nc + 1 - core) * capacity + slot) * CUT + cut

    send = padded_gradient(
        target, cot_here, cot_other, act_here, act_other, nx * nc, ny, capacity
    ).astype(jnp.float16)
    send = send.reshape(nx * nc, ny * pairs, 2 * capacity, half)
    send, target_here, rank, key_here, key_other = lax.optimization_barrier(
        (send, target_here[:, None], rank, key_here[None, :], key_other[None, :])
    )
    got = lax.all_to_all(send, ("x", "c"), 0, 0, tiled=True)
    got = got.reshape(nx, nc, ny * pairs, 2 * capacity, half)
    send = jnp.sum(got.astype(jnp.float32), axis=0).astype(jnp.float16)
    got = lax.all_to_all(jnp.swapaxes(send, 0, 1), ("y", "zh"), 0, 0, tiled=True)
    got = got.reshape(ny, pairs, nc, 2, capacity, half)
    summed = jnp.sum(got.astype(jnp.float32), axis=0) * 2.0
    moment_new, second_new, master_new, low = adam_rows(
        side, rank, summed, first_moment[0, 0], block_second[0, 0], master_rows[0, 0]
    )

    low = copies_to_all(copies_to_all(low.astype(jnp.bfloat16), "y"), "x")
    low = low.reshape(-1, width // CUT)
    low_other = lax.ppermute(low, "c", SWAP)
    placed = place_rows(target_here, key_here, low)
    new_weight = place_rows(target_here, key_other, low_other, placed)
    return (new_weight, moment_new[None, None], second_new[None], master_new[None, None])


def solution(mesh):
    dp, mp = ("x", "y", "c"), ("zh", "zl")
    fine = Mesh(mesh.devices.reshape(GRID + (-1, PAIR)), dp + mp)
    return jax.shard_map(
        body,
        mesh=fine,
        in_specs=(
            P(dp, mp),
            P(dp, mp),
            P(),
            P(),
            P(mp, dp, None, None),
            P(mp, dp, None),
            P(mp, dp, None, None),
        ),
        out_specs=(
            P(mp, None),
            P(mp, dp, None, None),
            P(mp, dp, None),
            P(mp, dp, None, None),
        ),
        check_vma=False,
    )
```

```python
from functools import partial

import jax
import jax.numpy as jnp
from jax import lax
from jax.experimental import pallas as pl
from jax.experimental.pallas import tpu as pltpu
from jax.sharding import Mesh, PartitionSpec as P

HD = 128
GRID = (4, 8, 2)
PAIR = 2
CUT = 2


beta_one = 0.9
beta_two = 0.95
learn_rate = 0.05
decay_rate = 0.1
epsilon = 1e-08
fix_one = 1.0 - 0.9**10
fix_two = 1.0 - 0.95**10


def block_tables(starts, owners, capacity):
    neuron_ids = jnp.arange(HD, dtype=jnp.int32)
    count_blocks = starts.shape[0]
    block_ids = jnp.sum((starts[None, :] <= neuron_ids[:, None]).astype(jnp.int32), axis=1) - 1
    onehot = block_ids[:, None] == jnp.arange(count_blocks, dtype=jnp.int32)[None, :]
    row_owner = jnp.sum(jnp.where(onehot, owners[None, :], 0), axis=1)
    earlier = (row_owner[:, None] == row_owner[None, :]) & (
        neuron_ids[None, :] < neuron_ids[:, None]
    )
    row_slot = jnp.sum(earlier.astype(jnp.int32), axis=1)
    before_blocks = (owners[:, None] == owners[None, :]) & (starts[None, :] < starts[:, None])
    block_rank = jnp.sum(before_blocks.astype(jnp.int32), axis=1)
    row_rank = jnp.sum(jnp.where(onehot, block_rank[None, :], 0), axis=1)
    return row_owner * capacity + row_slot, row_rank


def adam_kernel(side_ref, rank_ref, sums_ref, moment_ref, second_ref, master_ref, *outs):
    moment_out, second_out, master_out, rows_out = outs
    even = side_ref[0] == 0
    capacity, width = moment_ref.shape
    half = sums_ref.shape[-1]
    blocks = width // (2 * half)
    low = lambda j: sums_ref[j // 2, 0, j % 2]
    high = lambda j: sums_ref[j // 2, 1, 1 - j % 2]
    slots = lax.broadcasted_iota(jnp.int32, (capacity, 1), 0)
    rank = sum(jnp.where(slots == slot, rank_ref[slot], 0) for slot in range(capacity))
    grads = []
    for block in range(blocks):
        grads.append(jnp.where(even, low(block), low((block - 1) % blocks)))
        grads.append(jnp.where(even, high((block + 1) % blocks), high(block)))
    squares = sum(jnp.sum(grad * grad, axis=1, keepdims=True) for grad in grads)
    slot_second = jnp.ones((capacity, 1), jnp.float32)
    for slot in range(2):
        here = rank == slot
        count = jnp.sum(jnp.where(here, float(width), 0.0), axis=0, keepdims=True)
        mean = jnp.sum(jnp.where(here, squares, 0.0), axis=0, keepdims=True) / jnp.maximum(count, 1.0)
        fresh = beta_two * second_ref[:, slot : slot + 1] + (1.0 - beta_two) * mean
        fresh = jnp.where(count > 0.0, fresh, 0.0)
        second_out[:, slot : slot + 1] = fresh
        slot_second = jnp.where(here, fresh, slot_second)
    filled = rank >= 0
    scale = 1.0 / (fix_one * (jnp.sqrt(slot_second / fix_two) + epsilon))
    for part, grad in enumerate(grads):
        span = slice(part * half, (part + 1) * half)
        moment = jnp.where(filled, beta_one * moment_ref[:, span] + (1.0 - beta_one) * grad, 0.0)
        master = master_ref[:, span]
        master = master - learn_rate * (moment * scale + decay_rate * master)
        master = jnp.where(filled, master, 0.0)
        moment_out[:, span] = moment
        master_out[:, span] = master
        piece, place = divmod(part * half, width // CUT)
        rows_out[piece * capacity : (piece + 1) * capacity, place : place + half] = master


def adam_rows(side, rank, sums, moment, second, master):
    capacity, width = moment.shape
    shape = lambda *dims: jax.ShapeDtypeStruct(dims, jnp.float32)
    vmem = pl.BlockSpec(memory_space=pltpu.VMEM)
    return pl.pallas_call(
        adam_kernel,
        in_specs=[pl.BlockSpec(memory_space=pltpu.SMEM)] * 2 + [vmem] * 4,
        out_specs=[vmem] * 4,
        out_shape=[
            shape(capacity, width),
            shape(1, 2),
            shape(capacity, width),
            shape(capacity * CUT, width // CUT),
        ],
        compiler_params=pltpu.CompilerParams(vmem_limit_bytes=32 * 2**20),
    )(side[None], rank, sums, moment, second[None], master)


SWAP = [(0, 1), (1, 0)]


def copies_to_all(block, axis):
    count = lax.axis_size(axis)
    return lax.all_to_all(jnp.broadcast_to(block[None], (count,) + block.shape), axis, 0, 0, tiled=True)


TOKEN_DOT = (((0,), (0,)), ((), ()))
PARAMS = pltpu.CompilerParams(vmem_limit_bytes=32 * 2**20)


def cost(flops, moved):
    return pl.CostEstimate(flops=flops, bytes_accessed=moved, transcendentals=0)


def copies_kernel(block_ref, out_ref, sems):
    copies = [
        pltpu.make_async_copy(block_ref, out_ref.at[i], sems.at[i]) for i in range(out_ref.shape[0])
    ]
    for copy in copies:
        copy.start()
    for copy in copies:
        copy.wait()


def copies_in_hbm(block, count):
    whole = pl.BlockSpec(memory_space=pl.ANY)
    return pl.pallas_call(
        copies_kernel,
        in_specs=[whole],
        out_specs=whole,
        out_shape=jax.ShapeDtypeStruct((count,) + block.shape, block.dtype),
        scratch_shapes=[pltpu.SemaphoreType.DMA((count,))],
        cost_estimate=cost(0, 2**20),
    )(block)


def first_kernel(cot_ref, act_ref, out_ref):
    for head in range(cot_ref.shape[0]):
        out_ref[head] = lax.dot_general(
            cot_ref[head], act_ref[...], TOKEN_DOT, preferred_element_type=jnp.float32
        )


def padded_kernel(target_ref, first_ref, here_ref, other_ref, own_ref, near_ref, far_ref, out_ref):
    lines, spots, heads, rows, half = out_ref.shape
    count, cores, capacity = lines * spots * rows, GRID[2], rows // 2
    row = lax.broadcasted_iota(jnp.int32, (count, HD), 0)
    line, spot = row // (spots * rows), row // rows % spots
    owner = (line // cores * spots + spot) * cores + line % cores
    slot, part_of = owner * capacity + row % capacity, row // capacity % 2
    dot = partial(lax.dot_general, dimension_numbers=TOKEN_DOT, preferred_element_type=jnp.float32)
    for head in range(heads):
        taken = slot == target_ref[head]
        own = first_ref[head] + dot(other_ref[head], own_ref[...])
        near = dot(here_ref[head], near_ref[...]) + dot(other_ref[head], far_ref[...])
        padded = jnp.zeros((count, half), jnp.float32)
        for part, grad in enumerate((own, near)):
            high = grad.astype(jnp.bfloat16)
            low = (grad - high.astype(jnp.float32)).astype(jnp.bfloat16)
            pick = jnp.where(taken & (part_of == part), 0.5, 0.0).astype(jnp.bfloat16)
            padded += jnp.dot(
                jnp.concatenate([pick, pick], axis=1),
                jnp.concatenate([high, low], axis=0),
                preferred_element_type=jnp.float32,
            )
        out_ref[:, :, head] = padded.reshape(lines, spots, rows, half)


def padded_gradient(target, cot_here, cot_other, act_here, act_other, lines, spots, capacity):
    heads, tokens, _ = cot_here.shape
    half = act_here[0].shape[1]
    vmem = pl.BlockSpec(memory_space=pltpu.VMEM)
    first = pl.pallas_call(
        first_kernel,
        in_specs=[vmem] * 2,
        out_specs=vmem,
        out_shape=jax.ShapeDtypeStruct((heads, HD, half), jnp.float32),
        compiler_params=PARAMS,
        cost_estimate=cost(2 * heads * tokens * HD * half, 2**20),
    )(cot_here, act_here[0])
    return pl.pallas_call(
        padded_kernel,
        in_specs=[vmem] * 7,
        out_specs=vmem,
        out_shape=jax.ShapeDtypeStruct((lines, spots, heads, 2 * capacity, half), jnp.float32),
        compiler_params=PARAMS,
        cost_estimate=cost(10 * heads * tokens * HD * half, 4 * 2**20),
    )(target[:, None, :], first, cot_here, cot_other, act_other[0], act_here[1], act_other[1])


def place_kernel(target_ref, key_ref, rows_ref, *refs):
    want = target_ref[...] * CUT + pl.program_id(0)
    pick = jnp.where(want == key_ref[...], 1.0, 0.0).astype(jnp.bfloat16)
    placed = jnp.dot(pick, rows_ref[...], preferred_element_type=jnp.float32)
    for ref in refs[:-1]:
        placed += ref[...].astype(jnp.float32)
    refs[-1][...] = placed.astype(jnp.bfloat16)


def place_rows(target, key, rows, *placed):
    count, piece = rows.shape
    whole = lambda shape: pl.BlockSpec(shape, lambda j: (0, 0))
    piece_spec = pl.BlockSpec((HD, piece), lambda j: (0, j))
    return pl.pallas_call(
        place_kernel,
        grid=(CUT,),
        in_specs=[whole((HD, 1)), whole((1, count)), whole((count, piece))] + [piece_spec] * len(placed),
        out_specs=piece_spec,
        out_shape=jax.ShapeDtypeStruct((HD, CUT * piece), jnp.bfloat16),
        compiler_params=PARAMS,
        cost_estimate=cost(2 * CUT * HD * count * piece, 2 * 2**20),
    )(target, key, rows, *placed)


def body(activations, cotangent, block_start, block_owner, first_moment, block_second, master_rows):
    nx, ny, nc = GRID
    capacity, width = first_moment.shape[2], first_moment.shape[3]
    chips = nx * ny
    core, side, pair = lax.axis_index("c"), lax.axis_index("zl"), lax.axis_index("zh")
    pairs = lax.axis_size("zh")
    chip = lax.axis_index("x") * ny + lax.axis_index("y")
    owner_here = chip * nc + core
    half = activations.shape[1] // 2

    cot_here = lax.all_to_all(copies_in_hbm(cotangent, pairs), "zh", 0, 0, tiled=True)
    def of_side(table):
        return lax.dynamic_index_in_dim(table.reshape(pairs, PAIR, -1), side, 1, keepdims=False)

    target, row_rank = jax.vmap(partial(block_tables, capacity=capacity))(
        of_side(block_start), of_side(block_owner)
    )
    target, activations = lax.optimization_barrier((target, activations))
    keep = lax.dynamic_slice_in_dim(activations, core * half, half, 1)
    give = lax.dynamic_slice_in_dim(activations, (1 - core) * half, half, 1)
    depth = PAIR * pairs
    to_chip = lambda core_to, z: core_to * depth + (z + 2 * core_to - 1) % depth
    same = [(c * depth + z, to_chip(c, z)) for c in range(nc) for z in range(depth)]
    cross = [(c * depth + z, to_chip(1 - c, z)) for c in range(nc) for z in range(depth)]
    act_here = (keep, lax.ppermute(keep, ("c", "zh", "zl"), same))
    act_other = (lax.ppermute(give, "c", SWAP), lax.ppermute(give, ("c", "zh", "zl"), cross))
    cot_other = lax.ppermute(cot_here, "c", SWAP)

    target_here = lax.dynamic_index_in_dim(target, pair, 0, keepdims=False)
    rank_here = lax.dynamic_index_in_dim(row_rank, pair, 0, keepdims=False)
    slot_ids = owner_here * capacity + jnp.arange(capacity, dtype=jnp.int32)
    mine = slot_ids[:, None] == target_here[None, :]
    rank = jnp.max(jnp.where(mine, rank_here[None, :], -1), axis=1)
    row = jnp.arange(chips * capacity * CUT, dtype=jnp.int32)
    from_chip, cut, slot = row // (capacity * CUT), row // capacity % CUT, row % capacity
    key_here = ((from_chip * nc + core) * capacity + slot) * CUT + cut
    key_other = ((from_chip * nc + 1 - core) * capacity + slot) * CUT + cut

    send = padded_gradient(
        target, cot_here, cot_other, act_here, act_other, nx * nc, ny, capacity
    ).astype(jnp.float16)
    send = send.reshape(nx * nc, ny * pairs, 2 * capacity, half)
    send, target_here, rank, key_here, key_other = lax.optimization_barrier(
        (send, target_here[:, None], rank, key_here[None, :], key_other[None, :])
    )
    got = lax.all_to_all(send, ("x", "c"), 0, 0, tiled=True)
    got = got.reshape(nx, nc, ny * pairs, 2 * capacity, half)
    send = jnp.sum(got.astype(jnp.float32), axis=0).astype(jnp.float16)
    got = lax.all_to_all(jnp.swapaxes(send, 0, 1), ("y", "zh"), 0, 0, tiled=True)
    got = got.reshape(ny, pairs, nc, 2, capacity, half)
    summed = jnp.sum(got.astype(jnp.float32), axis=0) * 2.0
    moment_new, second_new, master_new, low = adam_rows(
        side, rank, summed, first_moment[0, 0], block_second[0, 0], master_rows[0, 0]
    )

    low = copies_to_all(copies_to_all(low.astype(jnp.bfloat16), "y"), "x")
    low = low.reshape(-1, width // CUT)
    low_other = lax.ppermute(low, "c", SWAP)
    placed = place_rows(target_here, key_here, low)
    new_weight = place_rows(target_here, key_other, low_other, placed)
    return (new_weight, moment_new[None, None], second_new[None], master_new[None, None])


def solution(mesh):
    dp, mp = ("x", "y", "c"), ("zh", "zl")
    fine = Mesh(mesh.devices.reshape(GRID + (-1, PAIR)), dp + mp)
    return jax.shard_map(
        body,
        mesh=fine,
        in_specs=(
            P(dp, mp),
            P(dp, mp),
            P(),
            P(),
            P(mp, dp, None, None),
            P(mp, dp, None),
            P(mp, dp, None, None),
        ),
        out_specs=(
            P(mp, None),
            P(mp, dp, None, None),
            P(mp, dp, None),
            P(mp, dp, None, None),
        ),
        check_vma=False,
    )
```

```python
from functools import partial

import jax
import jax.numpy as jnp
from jax import lax
from jax.experimental import pallas as pl
from jax.experimental.pallas import tpu as pltpu
from jax.sharding import Mesh, PartitionSpec as P

HD = 128
GRID = (4, 8, 2)
PAIR = 2
CUT = 2


beta_one = 0.9
beta_two = 0.95
learn_rate = 0.05
decay_rate = 0.1
epsilon = 1e-08
fix_one = 1.0 - 0.9**10
fix_two = 1.0 - 0.95**10


def block_tables(starts, owners, capacity):
    neuron_ids = jnp.arange(HD, dtype=jnp.int32)
    count_blocks = starts.shape[0]
    block_ids = jnp.sum((starts[None, :] <= neuron_ids[:, None]).astype(jnp.int32), axis=1) - 1
    onehot = block_ids[:, None] == jnp.arange(count_blocks, dtype=jnp.int32)[None, :]
    row_owner = jnp.sum(jnp.where(onehot, owners[None, :], 0), axis=1)
    earlier = (row_owner[:, None] == row_owner[None, :]) & (
        neuron_ids[None, :] < neuron_ids[:, None]
    )
    row_slot = jnp.sum(earlier.astype(jnp.int32), axis=1)
    before_blocks = (owners[:, None] == owners[None, :]) & (starts[None, :] < starts[:, None])
    block_rank = jnp.sum(before_blocks.astype(jnp.int32), axis=1)
    row_rank = jnp.sum(jnp.where(onehot, block_rank[None, :], 0), axis=1)
    return row_owner * capacity + row_slot, row_rank


def adam_kernel(side_ref, rank_ref, sums_ref, moment_ref, second_ref, master_ref, *outs):
    grad_out, scale_out, second_out, rows_out = outs
    even = side_ref[0] == 0
    capacity, width = moment_ref.shape
    half = sums_ref.shape[-1]
    blocks = width // (2 * half)
    low = lambda j: sums_ref[j // 2, 0, j % 2]
    high = lambda j: sums_ref[j // 2, 1, 1 - j % 2]
    slots = lax.broadcasted_iota(jnp.int32, (capacity, 1), 0)
    rank = sum(jnp.where(slots == slot, rank_ref[slot], 0) for slot in range(capacity))
    grads = []
    for block in range(blocks):
        grads.append(jnp.where(even, low(block), low((block - 1) % blocks)))
        grads.append(jnp.where(even, high((block + 1) % blocks), high(block)))
    squares = sum(jnp.sum(grad * grad, axis=1, keepdims=True) for grad in grads)
    slot_second = jnp.ones((capacity, 1), jnp.float32)
    for slot in range(2):
        here = rank == slot
        count = jnp.sum(jnp.where(here, float(width), 0.0), axis=0, keepdims=True)
        mean = jnp.sum(jnp.where(here, squares, 0.0), axis=0, keepdims=True) / jnp.maximum(count, 1.0)
        fresh = beta_two * second_ref[:, slot : slot + 1] + (1.0 - beta_two) * mean
        fresh = jnp.where(count > 0.0, fresh, 0.0)
        second_out[:, slot : slot + 1] = fresh
        slot_second = jnp.where(here, fresh, slot_second)
    filled = rank >= 0
    scale = 1.0 / (fix_one * (jnp.sqrt(slot_second / fix_two) + epsilon))
    scale_out[...] = scale
    for part, grad in enumerate(grads):
        span = slice(part * half, (part + 1) * half)
        moment = jnp.where(filled, beta_one * moment_ref[:, span] + (1.0 - beta_one) * grad, 0.0)
        master = master_ref[:, span]
        master = master - learn_rate * (moment * scale + decay_rate * master)
        master = jnp.where(filled, master, 0.0)
        grad_out[:, span] = grad
        piece, place = divmod(part * half, width // CUT)
        rows_out[piece * capacity : (piece + 1) * capacity, place : place + half] = master


def adam_rows(side, rank, sums, moment, second, master):
    capacity, width = moment.shape
    shape = lambda *dims: jax.ShapeDtypeStruct(dims, jnp.float32)
    vmem = pl.BlockSpec(memory_space=pltpu.VMEM)
    return pl.pallas_call(
        adam_kernel,
        in_specs=[pl.BlockSpec(memory_space=pltpu.SMEM)] * 2 + [vmem] * 4,
        out_specs=[vmem] * 4,
        out_shape=[
            shape(capacity, width),
            shape(capacity, 1),
            shape(1, 2),
            shape(capacity * CUT, width // CUT),
        ],
        compiler_params=pltpu.CompilerParams(vmem_limit_bytes=32 * 2**20),
    )(side[None], rank, sums, moment, second[None], master)


SWAP = [(0, 1), (1, 0)]


def copies_to_all(block, axis):
    count = lax.axis_size(axis)
    return lax.all_to_all(jnp.broadcast_to(block[None], (count,) + block.shape), axis, 0, 0, tiled=True)


TOKEN_DOT = (((0,), (0,)), ((), ()))
PARAMS = pltpu.CompilerParams(vmem_limit_bytes=32 * 2**20)


def cost(flops, moved):
    return pl.CostEstimate(flops=flops, bytes_accessed=moved, transcendentals=0)


def copies_kernel(block_ref, out_ref, sems):
    copies = [
        pltpu.make_async_copy(block_ref, out_ref.at[i], sems.at[i]) for i in range(out_ref.shape[0])
    ]
    for copy in copies:
        copy.start()
    for copy in copies:
        copy.wait()


def copies_in_hbm(block, count):
    return pl.pallas_call(
        copies_kernel,
        in_specs=[pl.BlockSpec(memory_space=pltpu.VMEM)],
        out_specs=pl.BlockSpec(memory_space=pl.ANY),
        out_shape=jax.ShapeDtypeStruct((count,) + block.shape, block.dtype),
        scratch_shapes=[pltpu.SemaphoreType.DMA((count,))],
        cost_estimate=cost(0, 2**20),
    )(block)


def first_kernel(cot_ref, act_ref, out_ref):
    for head in range(cot_ref.shape[0]):
        out_ref[head] = lax.dot_general(
            cot_ref[head], act_ref[...], TOKEN_DOT, preferred_element_type=jnp.float32
        )


def padded_kernel(target_ref, first_ref, here_ref, other_ref, own_ref, near_ref, far_ref, out_ref):
    lines, spots, heads, rows, half = out_ref.shape
    count, cores, capacity = lines * spots * rows, GRID[2], rows // 2
    row = lax.broadcasted_iota(jnp.int32, (count, HD), 0)
    line, spot = row // (spots * rows), row // rows % spots
    owner = (line // cores * spots + spot) * cores + line % cores
    slot, part_of = owner * capacity + row % capacity, row // capacity % 2
    dot = partial(lax.dot_general, dimension_numbers=TOKEN_DOT, preferred_element_type=jnp.float32)
    for head in range(heads):
        taken = slot == target_ref[head]
        own = first_ref[head] + dot(other_ref[head], own_ref[...])
        near = dot(here_ref[head], near_ref[...]) + dot(other_ref[head], far_ref[...])
        padded = jnp.zeros((count, half), jnp.float32)
        for part, grad in enumerate((own, near)):
            high = grad.astype(jnp.bfloat16)
            low = (grad - high.astype(jnp.float32)).astype(jnp.bfloat16)
            pick = jnp.where(taken & (part_of == part), 0.5, 0.0).astype(jnp.bfloat16)
            padded += jnp.dot(
                jnp.concatenate([pick, pick], axis=1),
                jnp.concatenate([high, low], axis=0),
                preferred_element_type=jnp.float32,
            )
        out_ref[:, :, head] = padded.reshape(lines, spots, rows, half)


def padded_gradient(target, cot_here, cot_other, act_here, act_other, lines, spots, capacity):
    heads, tokens, _ = cot_here.shape
    half = act_here[0].shape[1]
    vmem = pl.BlockSpec(memory_space=pltpu.VMEM)
    first = pl.pallas_call(
        first_kernel,
        in_specs=[vmem] * 2,
        out_specs=vmem,
        out_shape=jax.ShapeDtypeStruct((heads, HD, half), jnp.float32),
        compiler_params=PARAMS,
        cost_estimate=cost(2 * heads * tokens * HD * half, 2**20),
    )(cot_here, act_here[0])
    return pl.pallas_call(
        padded_kernel,
        in_specs=[vmem] * 7,
        out_specs=vmem,
        out_shape=jax.ShapeDtypeStruct((lines, spots, heads, 2 * capacity, half), jnp.float32),
        compiler_params=PARAMS,
        cost_estimate=cost(10 * heads * tokens * HD * half, 4 * 2**20),
    )(target[:, None, :], first, cot_here, cot_other, act_other[0], act_here[1], act_other[1])


def place_kernel(target_ref, key_ref, rows_ref, *refs):
    want = target_ref[...] * CUT + pl.program_id(0)
    pick = jnp.where(want == key_ref[...], 1.0, 0.0).astype(jnp.bfloat16)
    placed = jnp.dot(pick, rows_ref[...], preferred_element_type=jnp.float32)
    for ref in refs[:-1]:
        placed += ref[...].astype(jnp.float32)
    refs[-1][...] = placed.astype(jnp.bfloat16)


def place_rows(target, key, rows, *placed):
    count, piece = rows.shape
    whole = lambda shape: pl.BlockSpec(shape, lambda j: (0, 0))
    piece_spec = pl.BlockSpec((HD, piece), lambda j: (0, j))
    return pl.pallas_call(
        place_kernel,
        grid=(CUT,),
        in_specs=[whole((HD, 1)), whole((1, count)), whole((count, piece))] + [piece_spec] * len(placed),
        out_specs=piece_spec,
        out_shape=jax.ShapeDtypeStruct((HD, CUT * piece), jnp.bfloat16),
        compiler_params=PARAMS,
        cost_estimate=cost(2 * CUT * HD * count * piece, 2 * 2**20),
    )(target, key, rows, *placed)


def body(activations, cotangent, block_start, block_owner, first_moment, block_second, master_rows):
    nx, ny, nc = GRID
    capacity, width = first_moment.shape[2], first_moment.shape[3]
    chips = nx * ny
    core, side, pair = lax.axis_index("c"), lax.axis_index("zl"), lax.axis_index("zh")
    pairs = lax.axis_size("zh")
    chip = lax.axis_index("x") * ny + lax.axis_index("y")
    owner_here = chip * nc + core
    half = activations.shape[1] // 2

    cot_here = lax.all_to_all(copies_in_hbm(cotangent, pairs), "zh", 0, 0, tiled=True)
    def of_side(table):
        return lax.dynamic_index_in_dim(table.reshape(pairs, PAIR, -1), side, 1, keepdims=False)

    target, row_rank = jax.vmap(partial(block_tables, capacity=capacity))(
        of_side(block_start), of_side(block_owner)
    )
    target, activations = lax.optimization_barrier((target, activations))
    keep = lax.dynamic_slice_in_dim(activations, core * half, half, 1)
    give = lax.dynamic_slice_in_dim(activations, (1 - core) * half, half, 1)
    depth = PAIR * pairs
    to_chip = lambda core_to, z: core_to * depth + (z + 2 * core_to - 1) % depth
    same = [(c * depth + z, to_chip(c, z)) for c in range(nc) for z in range(depth)]
    cross = [(c * depth + z, to_chip(1 - c, z)) for c in range(nc) for z in range(depth)]
    act_here = (keep, lax.ppermute(keep, ("c", "zh", "zl"), same))
    act_other = (lax.ppermute(give, "c", SWAP), lax.ppermute(give, ("c", "zh", "zl"), cross))
    cot_other = lax.ppermute(cot_here, "c", SWAP)

    target_here = lax.dynamic_index_in_dim(target, pair, 0, keepdims=False)
    rank_here = lax.dynamic_index_in_dim(row_rank, pair, 0, keepdims=False)
    slot_ids = owner_here * capacity + jnp.arange(capacity, dtype=jnp.int32)
    mine = slot_ids[:, None] == target_here[None, :]
    rank = jnp.max(jnp.where(mine, rank_here[None, :], -1), axis=1)
    row = jnp.arange(chips * capacity * CUT, dtype=jnp.int32)
    from_chip, cut, slot = row // (capacity * CUT), row // capacity % CUT, row % capacity
    key_here = ((from_chip * nc + core) * capacity + slot) * CUT + cut
    key_other = ((from_chip * nc + 1 - core) * capacity + slot) * CUT + cut

    send = padded_gradient(
        target, cot_here, cot_other, act_here, act_other, nx * nc, ny, capacity
    ).astype(jnp.float16)
    send = send.reshape(nx * nc, ny * pairs, 2 * capacity, half)
    send, target_here, rank, key_here, key_other = lax.optimization_barrier(
        (send, target_here[:, None], rank, key_here[None, :], key_other[None, :])
    )
    got = lax.all_to_all(send, ("x", "c"), 0, 0, tiled=True)
    got = got.reshape(nx, nc, ny * pairs, 2 * capacity, half)
    send = jnp.sum(got.astype(jnp.float32), axis=0).astype(jnp.float16)
    got = lax.all_to_all(jnp.swapaxes(send, 0, 1), ("y", "zh"), 0, 0, tiled=True)
    got = got.reshape(ny, pairs, nc, 2, capacity, half)
    summed = jnp.sum(got.astype(jnp.float32), axis=0) * 2.0
    moment, master = first_moment[0, 0], master_rows[0, 0]
    grads, scale, second_new, low = adam_rows(side, rank, summed, moment, block_second[0, 0], master)

    low = copies_to_all(copies_to_all(low.astype(jnp.bfloat16), "y"), "x")
    low = low.reshape(-1, width // CUT)
    low, grads, scale, second_new, target_here, rank = lax.optimization_barrier(
        (low, grads, scale, second_new, target_here, rank)
    )
    filled = (rank >= 0)[:, None]
    moment_new = jnp.where(filled, beta_one * moment + (1.0 - beta_one) * grads, 0.0)
    master_new = master - learn_rate * (moment_new * scale + decay_rate * master)
    master_new = jnp.where(filled, master_new, 0.0)
    low_other = lax.ppermute(low, "c", SWAP)
    placed = place_rows(target_here, key_here, low)
    new_weight = place_rows(target_here, key_other, low_other, placed)
    return (new_weight, moment_new[None, None], second_new[None], master_new[None, None])


def solution(mesh):
    dp, mp = ("x", "y", "c"), ("zh", "zl")
    fine = Mesh(mesh.devices.reshape(GRID + (-1, PAIR)), dp + mp)
    return jax.shard_map(
        body,
        mesh=fine,
        in_specs=(
            P(dp, mp),
            P(dp, mp),
            P(),
            P(),
            P(mp, dp, None, None),
            P(mp, dp, None),
            P(mp, dp, None, None),
        ),
        out_specs=(
            P(mp, None),
            P(mp, dp, None, None),
            P(mp, dp, None),
            P(mp, dp, None, None),
        ),
        check_vma=False,
    )
```

```python
from functools import partial

import jax
import jax.numpy as jnp
from jax import lax
from jax.experimental import pallas as pl
from jax.experimental.pallas import tpu as pltpu
from jax.sharding import Mesh, PartitionSpec as P

HD = 128
GRID = (4, 8, 2)
PAIR = 2
CUT = 2


beta_one = 0.9
beta_two = 0.95
learn_rate = 0.05
decay_rate = 0.1
epsilon = 1e-08
fix_one = 1.0 - 0.9**10
fix_two = 1.0 - 0.95**10


def block_tables(starts, owners, capacity):
    neuron_ids = jnp.arange(HD, dtype=jnp.int32)
    count_blocks = starts.shape[0]
    block_ids = jnp.sum((starts[None, :] <= neuron_ids[:, None]).astype(jnp.int32), axis=1) - 1
    onehot = block_ids[:, None] == jnp.arange(count_blocks, dtype=jnp.int32)[None, :]
    row_owner = jnp.sum(jnp.where(onehot, owners[None, :], 0), axis=1)
    earlier = (row_owner[:, None] == row_owner[None, :]) & (
        neuron_ids[None, :] < neuron_ids[:, None]
    )
    row_slot = jnp.sum(earlier.astype(jnp.int32), axis=1)
    before_blocks = (owners[:, None] == owners[None, :]) & (starts[None, :] < starts[:, None])
    block_rank = jnp.sum(before_blocks.astype(jnp.int32), axis=1)
    row_rank = jnp.sum(jnp.where(onehot, block_rank[None, :], 0), axis=1)
    return row_owner * capacity + row_slot, row_rank


def adam_kernel(side_ref, rank_ref, sums_ref, moment_ref, second_ref, master_ref, *outs):
    grad_out, scale_out, second_out, rows_out = outs
    even = side_ref[0] == 0
    capacity, width = moment_ref.shape
    half = sums_ref.shape[-1]
    blocks = width // (2 * half)
    low = lambda j: sums_ref[j // 2, 0, j % 2]
    high = lambda j: sums_ref[j // 2, 1, 1 - j % 2]
    slots = lax.broadcasted_iota(jnp.int32, (capacity, 1), 0)
    rank = sum(jnp.where(slots == slot, rank_ref[slot], 0) for slot in range(capacity))
    grads = []
    for block in range(blocks):
        grads.append(jnp.where(even, low(block), low((block - 1) % blocks)))
        grads.append(jnp.where(even, high((block + 1) % blocks), high(block)))
    squares = sum(jnp.sum(grad * grad, axis=1, keepdims=True) for grad in grads)
    slot_second = jnp.ones((capacity, 1), jnp.float32)
    for slot in range(2):
        here = rank == slot
        count = jnp.sum(jnp.where(here, float(width), 0.0), axis=0, keepdims=True)
        mean = jnp.sum(jnp.where(here, squares, 0.0), axis=0, keepdims=True) / jnp.maximum(count, 1.0)
        fresh = beta_two * second_ref[:, slot : slot + 1] + (1.0 - beta_two) * mean
        fresh = jnp.where(count > 0.0, fresh, 0.0)
        second_out[:, slot : slot + 1] = fresh
        slot_second = jnp.where(here, fresh, slot_second)
    filled = rank >= 0
    scale = 1.0 / (fix_one * (jnp.sqrt(slot_second / fix_two) + epsilon))
    scale_out[...] = scale
    for part, grad in enumerate(grads):
        span = slice(part * half, (part + 1) * half)
        moment = jnp.where(filled, beta_one * moment_ref[:, span] + (1.0 - beta_one) * grad, 0.0)
        master = master_ref[:, span]
        master = master - learn_rate * (moment * scale + decay_rate * master)
        master = jnp.where(filled, master, 0.0)
        grad_out[:, span] = grad
        piece, place = divmod(part * half, width // CUT)
        rows_out[piece * capacity : (piece + 1) * capacity, place : place + half] = master


def adam_rows(side, rank, sums, moment, second, master):
    capacity, width = moment.shape
    shape = lambda *dims: jax.ShapeDtypeStruct(dims, jnp.float32)
    vmem = pl.BlockSpec(memory_space=pltpu.VMEM)
    return pl.pallas_call(
        adam_kernel,
        in_specs=[pl.BlockSpec(memory_space=pltpu.SMEM)] * 2 + [vmem] * 4,
        out_specs=[vmem] * 4,
        out_shape=[
            shape(capacity, width),
            shape(capacity, 1),
            shape(1, 2),
            shape(capacity * CUT, width // CUT),
        ],
        compiler_params=pltpu.CompilerParams(vmem_limit_bytes=32 * 2**20),
    )(side[None], rank, sums, moment, second[None], master)


SWAP = [(0, 1), (1, 0)]


def copies_to_all(block, axis):
    count = lax.axis_size(axis)
    return lax.all_to_all(jnp.broadcast_to(block[None], (count,) + block.shape), axis, 0, 0, tiled=True)


TOKEN_DOT = (((0,), (0,)), ((), ()))
PARAMS = pltpu.CompilerParams(vmem_limit_bytes=32 * 2**20)


def cost(flops, moved):
    return pl.CostEstimate(flops=flops, bytes_accessed=moved, transcendentals=0)


def copies_kernel(block_ref, out_ref, sems):
    copies = [
        pltpu.make_async_copy(block_ref, out_ref.at[i], sems.at[i]) for i in range(out_ref.shape[0])
    ]
    for copy in copies:
        copy.start()
    for copy in copies:
        copy.wait()


def copies_in_hbm(block, count):
    return pl.pallas_call(
        copies_kernel,
        in_specs=[pl.BlockSpec(memory_space=pltpu.VMEM)],
        out_specs=pl.BlockSpec(memory_space=pl.ANY),
        out_shape=jax.ShapeDtypeStruct((count,) + block.shape, block.dtype),
        scratch_shapes=[pltpu.SemaphoreType.DMA((count,))],
        cost_estimate=cost(0, 2**20),
    )(block)


def first_kernel(cot_ref, act_ref, out_ref):
    for head in range(cot_ref.shape[0]):
        out_ref[head] = lax.dot_general(
            cot_ref[head], act_ref[...], TOKEN_DOT, preferred_element_type=jnp.float32
        )


def padded_kernel(target_ref, first_ref, here_ref, other_ref, own_ref, near_ref, far_ref, out_ref):
    lines, spots, heads, rows, half = out_ref.shape
    count, cores, capacity = lines * spots * rows, GRID[2], rows // 2
    row = lax.broadcasted_iota(jnp.int32, (count, HD), 0)
    line, spot = row // (spots * rows), row // rows % spots
    owner = (line // cores * spots + spot) * cores + line % cores
    slot, part_of = owner * capacity + row % capacity, row // capacity % 2
    dot = partial(lax.dot_general, dimension_numbers=TOKEN_DOT, preferred_element_type=jnp.float32)
    for head in range(heads):
        taken = slot == target_ref[head]
        own = first_ref[head] + dot(other_ref[head], own_ref[...])
        near = dot(here_ref[head], near_ref[...]) + dot(other_ref[head], far_ref[...])
        padded = jnp.zeros((count, half), jnp.float32)
        for part, grad in enumerate((own, near)):
            high = grad.astype(jnp.bfloat16)
            low = (grad - high.astype(jnp.float32)).astype(jnp.bfloat16)
            pick = jnp.where(taken & (part_of == part), 0.5, 0.0).astype(jnp.bfloat16)
            padded += jnp.dot(
                jnp.concatenate([pick, pick], axis=1),
                jnp.concatenate([high, low], axis=0),
                preferred_element_type=jnp.float32,
            )
        out_ref[:, :, head] = padded.reshape(lines, spots, rows, half)


def padded_gradient(target, cot_here, cot_other, act_here, act_other, lines, spots, capacity):
    heads, tokens, _ = cot_here.shape
    half = act_here[0].shape[1]
    vmem = pl.BlockSpec(memory_space=pltpu.VMEM)
    first = pl.pallas_call(
        first_kernel,
        in_specs=[vmem] * 2,
        out_specs=vmem,
        out_shape=jax.ShapeDtypeStruct((heads, HD, half), jnp.float32),
        compiler_params=PARAMS,
        cost_estimate=cost(2 * heads * tokens * HD * half, 2**20),
    )(cot_here, act_here[0])
    return pl.pallas_call(
        padded_kernel,
        in_specs=[vmem] * 7,
        out_specs=vmem,
        out_shape=jax.ShapeDtypeStruct((lines, spots, heads, 2 * capacity, half), jnp.float32),
        compiler_params=PARAMS,
        cost_estimate=cost(10 * heads * tokens * HD * half, 4 * 2**20),
    )(target[:, None, :], first, cot_here, cot_other, act_other[0], act_here[1], act_other[1])


def place_kernel(target_ref, key_ref, rows_ref, *refs):
    want = target_ref[...] * CUT + pl.program_id(1)
    pick = jnp.where(want == key_ref[...], 1.0, 0.0).astype(jnp.bfloat16)
    placed = jnp.dot(pick, rows_ref[...], preferred_element_type=jnp.float32)
    for ref in refs[:-1]:
        placed += ref[...].astype(jnp.float32)
    refs[-1][...] = placed.astype(jnp.bfloat16)


def place_rows(target, key, rows, *placed):
    count, piece = rows.shape
    whole = lambda shape: pl.BlockSpec(shape, lambda i, j: (0, 0))
    parts = 2
    part = piece // parts
    part_spec = pl.BlockSpec((HD, part), lambda i, j: (0, j * parts + i))
    rows_spec = pl.BlockSpec((count, part), lambda i, j: (0, i))
    return pl.pallas_call(
        place_kernel,
        grid=(parts, CUT),
        in_specs=[whole((HD, 1)), whole((1, count)), rows_spec] + [part_spec] * len(placed),
        out_specs=part_spec,
        out_shape=jax.ShapeDtypeStruct((HD, CUT * piece), jnp.bfloat16),
        compiler_params=PARAMS,
        cost_estimate=cost(2 * CUT * HD * count * piece, 2 * 2**20),
    )(target, key, rows, *placed)


def body(activations, cotangent, block_start, block_owner, first_moment, block_second, master_rows):
    nx, ny, nc = GRID
    capacity, width = first_moment.shape[2], first_moment.shape[3]
    chips = nx * ny
    core, side, pair = lax.axis_index("c"), lax.axis_index("zl"), lax.axis_index("zh")
    pairs = lax.axis_size("zh")
    chip = lax.axis_index("x") * ny + lax.axis_index("y")
    owner_here = chip * nc + core
    half = activations.shape[1] // 2

    cot_here = lax.all_to_all(copies_in_hbm(cotangent, pairs), "zh", 0, 0, tiled=True)
    def of_side(table):
        return lax.dynamic_index_in_dim(table.reshape(pairs, PAIR, -1), side, 1, keepdims=False)

    target, row_rank = jax.vmap(partial(block_tables, capacity=capacity))(
        of_side(block_start), of_side(block_owner)
    )
    keep = lax.dynamic_slice_in_dim(activations, core * half, half, 1)
    target, activations = lax.optimization_barrier((target, activations))
    give = lax.dynamic_slice_in_dim(activations, (1 - core) * half, half, 1)
    depth = PAIR * pairs
    to_chip = lambda core_to, z: core_to * depth + (z + 2 * core_to - 1) % depth
    same = [(c * depth + z, to_chip(c, z)) for c in range(nc) for z in range(depth)]
    cross = [(c * depth + z, to_chip(1 - c, z)) for c in range(nc) for z in range(depth)]
    act_here = (keep, lax.ppermute(keep, ("c", "zh", "zl"), same))
    far = lax.ppermute(give, ("c", "zh", "zl"), cross)
    row_rank, give = lax.optimization_barrier((row_rank + 0 * target, give))
    act_other = (lax.ppermute(give, "c", SWAP), far)
    cot_other = lax.ppermute(cot_here, "c", SWAP)

    target_here = lax.dynamic_index_in_dim(target, pair, 0, keepdims=False)
    rank_here = lax.dynamic_index_in_dim(row_rank, pair, 0, keepdims=False)
    slot_ids = owner_here * capacity + jnp.arange(capacity, dtype=jnp.int32)
    mine = slot_ids[:, None] == target_here[None, :]
    rank = jnp.max(jnp.where(mine, rank_here[None, :], -1), axis=1)
    row = jnp.arange(chips * capacity * CUT, dtype=jnp.int32)
    from_chip, cut, slot = row // (capacity * CUT), row // capacity % CUT, row % capacity
    key_here = ((from_chip * nc + core) * capacity + slot) * CUT + cut
    key_other = ((from_chip * nc + 1 - core) * capacity + slot) * CUT + cut

    send = padded_gradient(
        target, cot_here, cot_other, act_here, act_other, nx * nc, ny, capacity
    ).astype(jnp.float16)
    send = send.reshape(nx * nc, ny * pairs, 2 * capacity, half)
    send, target_here, rank, key_here, key_other = lax.optimization_barrier(
        (send, target_here[:, None], rank, key_here[None, :], key_other[None, :])
    )
    got = lax.all_to_all(send, ("x", "c"), 0, 0, tiled=True)
    got = got.reshape(nx, nc, ny * pairs, 2 * capacity, half)
    send = jnp.sum(got.astype(jnp.float32), axis=0).astype(jnp.float16)
    got = lax.all_to_all(jnp.swapaxes(send, 0, 1), ("y", "zh"), 0, 0, tiled=True)
    got = got.reshape(ny, pairs, nc, 2, capacity, half)
    summed = jnp.sum(got.astype(jnp.float32), axis=0) * 2.0
    moment, master = first_moment[0, 0], master_rows[0, 0]
    grads, scale, second_new, low = adam_rows(side, rank, summed, moment, block_second[0, 0], master)

    low = copies_to_all(copies_to_all(low.astype(jnp.bfloat16), "y"), "x")
    low = low.reshape(-1, width // CUT)
    low, grads, scale, second_new, target_here, rank = lax.optimization_barrier(
        (low, grads, scale, second_new, target_here, rank)
    )
    filled = (rank >= 0)[:, None]
    moment_new = jnp.where(filled, beta_one * moment + (1.0 - beta_one) * grads, 0.0)
    master_new = master - learn_rate * (moment_new * scale + decay_rate * master)
    master_new = jnp.where(filled, master_new, 0.0)
    low_other = lax.ppermute(low, "c", SWAP)
    placed = place_rows(target_here, key_here, low)
    new_weight = place_rows(target_here, key_other, low_other, placed)
    return (new_weight, moment_new[None, None], second_new[None], master_new[None, None])


def solution(mesh):
    dp, mp = ("x", "y", "c"), ("zh", "zl")
    fine = Mesh(mesh.devices.reshape(GRID + (-1, PAIR)), dp + mp)
    return jax.shard_map(
        body,
        mesh=fine,
        in_specs=(
            P(dp, mp),
            P(dp, mp),
            P(),
            P(),
            P(mp, dp, None, None),
            P(mp, dp, None),
            P(mp, dp, None, None),
        ),
        out_specs=(
            P(mp, None),
            P(mp, dp, None, None),
            P(mp, dp, None),
            P(mp, dp, None, None),
        ),
        check_vma=False,
    )
```

```python
from functools import partial

import jax
import jax.numpy as jnp
from jax import lax
from jax.experimental import pallas as pl
from jax.experimental.pallas import tpu as pltpu
from jax.sharding import Mesh, PartitionSpec as P

HD = 128
GRID = (4, 8, 2)
PAIR = 2
CUT = 2


beta_one = 0.9
beta_two = 0.95
learn_rate = 0.05
decay_rate = 0.1
epsilon = 1e-08
fix_one = 1.0 - 0.9**10
fix_two = 1.0 - 0.95**10


def block_tables(starts, owners, capacity):
    neuron_ids = jnp.arange(HD, dtype=jnp.int32)
    count_blocks = starts.shape[0]
    block_ids = jnp.sum((starts[None, :] <= neuron_ids[:, None]).astype(jnp.int32), axis=1) - 1
    onehot = block_ids[:, None] == jnp.arange(count_blocks, dtype=jnp.int32)[None, :]
    row_owner = jnp.sum(jnp.where(onehot, owners[None, :], 0), axis=1)
    earlier = (row_owner[:, None] == row_owner[None, :]) & (
        neuron_ids[None, :] < neuron_ids[:, None]
    )
    row_slot = jnp.sum(earlier.astype(jnp.int32), axis=1)
    before_blocks = (owners[:, None] == owners[None, :]) & (starts[None, :] < starts[:, None])
    block_rank = jnp.sum(before_blocks.astype(jnp.int32), axis=1)
    row_rank = jnp.sum(jnp.where(onehot, block_rank[None, :], 0), axis=1)
    return row_owner * capacity + row_slot, row_rank


def adam_kernel(side_ref, rank_ref, sums_ref, moment_ref, second_ref, master_ref, *outs):
    grad_out, scale_out, second_out, rows_out = outs
    even = side_ref[0] == 0
    capacity, width = moment_ref.shape
    half = sums_ref.shape[-1]
    blocks = width // (2 * half)
    low = lambda j: sums_ref[j // 2, 0, j % 2]
    high = lambda j: sums_ref[j // 2, 1, 1 - j % 2]
    slots = lax.broadcasted_iota(jnp.int32, (capacity, 1), 0)
    rank = sum(jnp.where(slots == slot, rank_ref[slot], 0) for slot in range(capacity))
    grads = []
    for block in range(blocks):
        grads.append(jnp.where(even, low(block), low((block - 1) % blocks)))
        grads.append(jnp.where(even, high((block + 1) % blocks), high(block)))
    squares = sum(jnp.sum(grad * grad, axis=1, keepdims=True) for grad in grads)
    slot_second = jnp.ones((capacity, 1), jnp.float32)
    for slot in range(2):
        here = rank == slot
        count = jnp.sum(jnp.where(here, float(width), 0.0), axis=0, keepdims=True)
        mean = jnp.sum(jnp.where(here, squares, 0.0), axis=0, keepdims=True) / jnp.maximum(count, 1.0)
        fresh = beta_two * second_ref[:, slot : slot + 1] + (1.0 - beta_two) * mean
        fresh = jnp.where(count > 0.0, fresh, 0.0)
        second_out[:, slot : slot + 1] = fresh
        slot_second = jnp.where(here, fresh, slot_second)
    filled = rank >= 0
    scale = 1.0 / (fix_one * (jnp.sqrt(slot_second / fix_two) + epsilon))
    scale_out[...] = scale
    for part, grad in enumerate(grads):
        span = slice(part * half, (part + 1) * half)
        moment = jnp.where(filled, beta_one * moment_ref[:, span] + (1.0 - beta_one) * grad, 0.0)
        master = master_ref[:, span]
        master = master - learn_rate * (moment * scale + decay_rate * master)
        master = jnp.where(filled, master, 0.0)
        grad_out[:, span] = grad
        piece, place = divmod(part * half, width // CUT)
        rows_out[piece * capacity : (piece + 1) * capacity, place : place + half] = master


def adam_rows(side, rank, sums, moment, second, master):
    capacity, width = moment.shape
    shape = lambda *dims: jax.ShapeDtypeStruct(dims, jnp.float32)
    vmem = pl.BlockSpec(memory_space=pltpu.VMEM)
    return pl.pallas_call(
        adam_kernel,
        in_specs=[pl.BlockSpec(memory_space=pltpu.SMEM)] * 2 + [vmem] * 4,
        out_specs=[vmem] * 4,
        out_shape=[
            shape(capacity, width),
            shape(capacity, 1),
            shape(1, 2),
            shape(capacity * CUT, width // CUT),
        ],
        compiler_params=pltpu.CompilerParams(vmem_limit_bytes=32 * 2**20),
    )(side[None], rank, sums, moment, second[None], master)


SWAP = [(0, 1), (1, 0)]


def copies_to_all(block, axis):
    count = lax.axis_size(axis)
    return lax.all_to_all(jnp.broadcast_to(block[None], (count,) + block.shape), axis, 0, 0, tiled=True)


TOKEN_DOT = (((0,), (0,)), ((), ()))
PARAMS = pltpu.CompilerParams(vmem_limit_bytes=32 * 2**20)


def cost(flops, moved):
    return pl.CostEstimate(flops=flops, bytes_accessed=moved, transcendentals=0)


def first_kernel(cot_ref, act_ref, out_ref):
    for head in range(cot_ref.shape[0]):
        out_ref[head] = lax.dot_general(
            cot_ref[head], act_ref[...], TOKEN_DOT, preferred_element_type=jnp.float32
        )


def padded_kernel(target_ref, first_ref, here_ref, other_ref, own_ref, near_ref, far_ref, out_ref):
    lines, spots, heads, rows, half = out_ref.shape
    count, cores, capacity = lines * spots * rows, GRID[2], rows // 2
    row = lax.broadcasted_iota(jnp.int32, (count, HD), 0)
    line, spot = row // (spots * rows), row // rows % spots
    owner = (line // cores * spots + spot) * cores + line % cores
    slot, part_of = owner * capacity + row % capacity, row // capacity % 2
    dot = partial(lax.dot_general, dimension_numbers=TOKEN_DOT, preferred_element_type=jnp.float32)
    for head in range(heads):
        taken = slot == target_ref[head]
        own = first_ref[head] + dot(other_ref[head], own_ref[...])
        near = dot(here_ref[head], near_ref[...]) + dot(other_ref[head], far_ref[...])
        padded = jnp.zeros((count, half), jnp.float32)
        for part, grad in enumerate((own, near)):
            high = grad.astype(jnp.bfloat16)
            low = (grad - high.astype(jnp.float32)).astype(jnp.bfloat16)
            pick = jnp.where(taken & (part_of == part), 0.5, 0.0).astype(jnp.bfloat16)
            padded += jnp.dot(
                jnp.concatenate([pick, pick], axis=1),
                jnp.concatenate([high, low], axis=0),
                preferred_element_type=jnp.float32,
            )
        out_ref[:, :, head] = padded.reshape(lines, spots, rows, half)


def padded_gradient(target, cot_here, cot_other, act_here, act_other, lines, spots, capacity):
    heads, tokens, _ = cot_here.shape
    half = act_here[0].shape[1]
    vmem = pl.BlockSpec(memory_space=pltpu.VMEM)
    first = pl.pallas_call(
        first_kernel,
        in_specs=[vmem] * 2,
        out_specs=vmem,
        out_shape=jax.ShapeDtypeStruct((heads, HD, half), jnp.float32),
        compiler_params=PARAMS,
        cost_estimate=cost(2 * heads * tokens * HD * half, 2**20),
    )(cot_here, act_here[0])
    return pl.pallas_call(
        padded_kernel,
        in_specs=[vmem] * 7,
        out_specs=vmem,
        out_shape=jax.ShapeDtypeStruct((lines, spots, heads, 2 * capacity, half), jnp.float32),
        compiler_params=PARAMS,
        cost_estimate=cost(10 * heads * tokens * HD * half, 4 * 2**20),
    )(target[:, None, :], first, cot_here, cot_other, act_other[0], act_here[1], act_other[1])


def placed_part(target_ref, key_ref, rows_ref, cut, span):
    pick = jnp.where(target_ref[...] * CUT + cut == key_ref[...], 1.0, 0.0).astype(jnp.bfloat16)
    return jnp.dot(pick, rows_ref[:, span], preferred_element_type=jnp.float32)


def place_kernel(target_ref, key_ref, rows_ref, out_ref):
    piece = rows_ref.shape[1]
    for cut in range(CUT):
        part = placed_part(target_ref, key_ref, rows_ref, cut, slice(0, piece))
        out_ref[:, cut * piece : (cut + 1) * piece] = part.astype(jnp.bfloat16)


def merge_kernel(target_ref, key_ref, rows_ref, placed_ref, out_ref, parts_ref, sems):
    count, _, part = parts_ref.shape
    copies = []
    for i in range(count):
        place = i * part % rows_ref.shape[1]
        rows = placed_part(
            target_ref, key_ref, rows_ref, i * part // rows_ref.shape[1], slice(place, place + part)
        )
        span = slice(i * part, (i + 1) * part)
        parts_ref[i] = (rows + placed_ref[:, span].astype(jnp.float32)).astype(jnp.bfloat16)
        copies.append(pltpu.make_async_copy(parts_ref.at[i], out_ref.at[:, span], sems.at[i]))
        copies[-1].start()
    for copy in copies:
        copy.wait()


def place_rows(target, key, rows, *placed):
    count, piece = rows.shape
    width, parts = CUT * piece, 2 * CUT
    vmem = pl.BlockSpec(memory_space=pltpu.VMEM)
    scratch = [
        pltpu.VMEM((parts, HD, width // parts), jnp.bfloat16),
        pltpu.SemaphoreType.DMA((parts,)),
    ]
    return pl.pallas_call(
        merge_kernel if placed else place_kernel,
        in_specs=[vmem] * (3 + len(placed)),
        out_specs=pl.BlockSpec(memory_space=pl.ANY) if placed else vmem,
        out_shape=jax.ShapeDtypeStruct((HD, width), jnp.bfloat16),
        scratch_shapes=scratch if placed else [],
        compiler_params=PARAMS,
        cost_estimate=cost(2 * CUT * HD * count * piece, 2 * 2**20),
    )(target, key, rows, *placed)


def body(activations, cotangent, block_start, block_owner, first_moment, block_second, master_rows):
    nx, ny, nc = GRID
    capacity, width = first_moment.shape[2], first_moment.shape[3]
    chips = nx * ny
    core, side, pair = lax.axis_index("c"), lax.axis_index("zl"), lax.axis_index("zh")
    pairs = lax.axis_size("zh")
    chip = lax.axis_index("x") * ny + lax.axis_index("y")
    owner_here = chip * nc + core
    half = activations.shape[1] // 2

    cot_here = copies_to_all(cotangent, "zh")
    def of_side(table):
        return lax.dynamic_index_in_dim(table.reshape(pairs, PAIR, -1), side, 1, keepdims=False)

    target, row_rank = jax.vmap(partial(block_tables, capacity=capacity))(
        of_side(block_start), of_side(block_owner)
    )
    target, activations = lax.optimization_barrier((target, activations))
    keep = lax.dynamic_slice_in_dim(activations, core * half, half, 1)
    give = lax.dynamic_slice_in_dim(activations, (1 - core) * half, half, 1)
    depth = PAIR * pairs
    to_chip = lambda core_to, z: core_to * depth + (z + 2 * core_to - 1) % depth
    same = [(c * depth + z, to_chip(c, z)) for c in range(nc) for z in range(depth)]
    cross = [(c * depth + z, to_chip(1 - c, z)) for c in range(nc) for z in range(depth)]
    act_here = (keep, lax.ppermute(keep, ("c", "zh", "zl"), same))
    act_other = (lax.ppermute(give, "c", SWAP), lax.ppermute(give, ("c", "zh", "zl"), cross))
    cot_other = lax.ppermute(cot_here, "c", SWAP)

    target_here = lax.dynamic_index_in_dim(target, pair, 0, keepdims=False)
    rank_here = lax.dynamic_index_in_dim(row_rank, pair, 0, keepdims=False)
    slot_ids = owner_here * capacity + jnp.arange(capacity, dtype=jnp.int32)
    mine = slot_ids[:, None] == target_here[None, :]
    rank = jnp.max(jnp.where(mine, rank_here[None, :], -1), axis=1)
    row = jnp.arange(chips * capacity * CUT, dtype=jnp.int32)
    from_chip, cut, slot = row // (capacity * CUT), row // capacity % CUT, row % capacity
    key_here = ((from_chip * nc + core) * capacity + slot) * CUT + cut
    key_other = ((from_chip * nc + 1 - core) * capacity + slot) * CUT + cut

    send = padded_gradient(
        target, cot_here, cot_other, act_here, act_other, nx * nc, ny, capacity
    ).astype(jnp.float16)
    send = send.reshape(nx * nc, ny * pairs, 2 * capacity, half)
    send, target_here, rank, key_here, key_other = lax.optimization_barrier(
        (send, target_here[:, None], rank, key_here[None, :], key_other[None, :])
    )
    got = lax.all_to_all(send, ("x", "c"), 0, 0, tiled=True)
    got = got.reshape(nx, nc, ny * pairs, 2 * capacity, half)
    send = jnp.sum(got.astype(jnp.float32), axis=0).astype(jnp.float16)
    got = lax.all_to_all(jnp.swapaxes(send, 0, 1), ("y", "zh"), 0, 0, tiled=True)
    got = got.reshape(ny, pairs, nc, 2, capacity, half)
    summed = jnp.sum(got.astype(jnp.float32), axis=0) * 2.0
    moment, master = first_moment[0, 0], master_rows[0, 0]
    grads, scale, second_new, low = adam_rows(side, rank, summed, moment, block_second[0, 0], master)

    low = copies_to_all(copies_to_all(low.astype(jnp.bfloat16), "y"), "x")
    low = low.reshape(-1, width // CUT)
    low, grads, scale, second_new, target_here, rank = lax.optimization_barrier(
        (low, grads, scale, second_new, target_here, rank)
    )
    filled = (rank >= 0)[:, None]
    moment_new = jnp.where(filled, beta_one * moment + (1.0 - beta_one) * grads, 0.0)
    master_new = master - learn_rate * (moment_new * scale + decay_rate * master)
    master_new = jnp.where(filled, master_new, 0.0)
    low_other = lax.ppermute(low, "c", SWAP)
    placed = place_rows(target_here, key_here, low)
    new_weight = place_rows(target_here, key_other, low_other, placed)
    return (new_weight, moment_new[None, None], second_new[None], master_new[None, None])


def solution(mesh):
    dp, mp = ("x", "y", "c"), ("zh", "zl")
    fine = Mesh(mesh.devices.reshape(GRID + (-1, PAIR)), dp + mp)
    return jax.shard_map(
        body,
        mesh=fine,
        in_specs=(
            P(dp, mp),
            P(dp, mp),
            P(),
            P(),
            P(mp, dp, None, None),
            P(mp, dp, None),
            P(mp, dp, None, None),
        ),
        out_specs=(
            P(mp, None),
            P(mp, dp, None, None),
            P(mp, dp, None),
            P(mp, dp, None, None),
        ),
        check_vma=False,
    )
```

```python
from functools import partial

import jax
import jax.numpy as jnp
from jax import lax
from jax.experimental import pallas as pl
from jax.experimental.pallas import tpu as pltpu
from jax.sharding import Mesh, PartitionSpec as P

HD = 128
GRID = (4, 8, 2)
PAIR = 2
CUT = 2


beta_one = 0.9
beta_two = 0.95
learn_rate = 0.05
decay_rate = 0.1
epsilon = 1e-08
fix_one = 1.0 - 0.9**10
fix_two = 1.0 - 0.95**10


def block_tables(starts, owners, capacity):
    neuron_ids = jnp.arange(HD, dtype=jnp.int32)
    count_blocks = starts.shape[0]
    block_ids = jnp.sum((starts[None, :] <= neuron_ids[:, None]).astype(jnp.int32), axis=1) - 1
    onehot = block_ids[:, None] == jnp.arange(count_blocks, dtype=jnp.int32)[None, :]
    row_owner = jnp.sum(jnp.where(onehot, owners[None, :], 0), axis=1)
    earlier = (row_owner[:, None] == row_owner[None, :]) & (
        neuron_ids[None, :] < neuron_ids[:, None]
    )
    row_slot = jnp.sum(earlier.astype(jnp.int32), axis=1)
    before_blocks = (owners[:, None] == owners[None, :]) & (starts[None, :] < starts[:, None])
    block_rank = jnp.sum(before_blocks.astype(jnp.int32), axis=1)
    row_rank = jnp.sum(jnp.where(onehot, block_rank[None, :], 0), axis=1)
    return row_owner * capacity + row_slot, row_rank


def adam_kernel(side_ref, rank_ref, sums_ref, moment_ref, second_ref, master_ref, *outs):
    grad_out, scale_out, second_out, rows_out = outs
    even = side_ref[0] == 0
    capacity, width = moment_ref.shape
    half = sums_ref.shape[-1]
    blocks = width // (2 * half)
    low = lambda j: sums_ref[j // 2, 0, j % 2]
    high = lambda j: sums_ref[j // 2, 1, 1 - j % 2]
    slots = lax.broadcasted_iota(jnp.int32, (capacity, 1), 0)
    rank = sum(jnp.where(slots == slot, rank_ref[slot], 0) for slot in range(capacity))
    grads = []
    for block in range(blocks):
        grads.append(jnp.where(even, low(block), low((block - 1) % blocks)))
        grads.append(jnp.where(even, high((block + 1) % blocks), high(block)))
    squares = sum(jnp.sum(grad * grad, axis=1, keepdims=True) for grad in grads)
    slot_second = jnp.ones((capacity, 1), jnp.float32)
    for slot in range(2):
        here = rank == slot
        count = jnp.sum(jnp.where(here, float(width), 0.0), axis=0, keepdims=True)
        mean = jnp.sum(jnp.where(here, squares, 0.0), axis=0, keepdims=True) / jnp.maximum(count, 1.0)
        fresh = beta_two * second_ref[:, slot : slot + 1] + (1.0 - beta_two) * mean
        fresh = jnp.where(count > 0.0, fresh, 0.0)
        second_out[:, slot : slot + 1] = fresh
        slot_second = jnp.where(here, fresh, slot_second)
    filled = rank >= 0
    scale = 1.0 / (fix_one * (jnp.sqrt(slot_second / fix_two) + epsilon))
    scale_out[...] = scale
    for part, grad in enumerate(grads):
        span = slice(part * half, (part + 1) * half)
        moment = jnp.where(filled, beta_one * moment_ref[:, span] + (1.0 - beta_one) * grad, 0.0)
        master = master_ref[:, span]
        master = master - learn_rate * (moment * scale + decay_rate * master)
        master = jnp.where(filled, master, 0.0)
        grad_out[:, span] = grad
        piece, place = divmod(part * half, width // CUT)
        rows_out[piece * capacity : (piece + 1) * capacity, place : place + half] = master


def adam_rows(side, rank, sums, moment, second, master):
    capacity, width = moment.shape
    shape = lambda *dims: jax.ShapeDtypeStruct(dims, jnp.float32)
    vmem = pl.BlockSpec(memory_space=pltpu.VMEM)
    return pl.pallas_call(
        adam_kernel,
        in_specs=[pl.BlockSpec(memory_space=pltpu.SMEM)] * 2 + [vmem] * 4,
        out_specs=[vmem] * 4,
        out_shape=[
            shape(capacity, width),
            shape(capacity, 1),
            shape(1, 2),
            shape(capacity * CUT, width // CUT),
        ],
        compiler_params=pltpu.CompilerParams(vmem_limit_bytes=32 * 2**20),
    )(side[None], rank, sums, moment, second[None], master)


SWAP = [(0, 1), (1, 0)]


def copies_to_all(block, axis):
    count = lax.axis_size(axis)
    return lax.all_to_all(jnp.broadcast_to(block[None], (count,) + block.shape), axis, 0, 0, tiled=True)


TOKEN_DOT = (((0,), (0,)), ((), ()))
PARAMS = pltpu.CompilerParams(vmem_limit_bytes=32 * 2**20)


def cost(flops, moved):
    return pl.CostEstimate(flops=flops, bytes_accessed=moved, transcendentals=0)


def first_kernel(cot_ref, act_ref, out_ref):
    for head in range(cot_ref.shape[0]):
        out_ref[head] = lax.dot_general(
            cot_ref[head], act_ref[...], TOKEN_DOT, preferred_element_type=jnp.float32
        )


def padded_kernel(target_ref, first_ref, here_ref, other_ref, own_ref, near_ref, far_ref, out_ref):
    lines, spots, heads, rows, half = out_ref.shape
    count, cores, capacity = lines * spots * rows, GRID[2], rows // 2
    row = lax.broadcasted_iota(jnp.int32, (count, HD), 0)
    line, spot = row // (spots * rows), row // rows % spots
    owner = (line // cores * spots + spot) * cores + line % cores
    slot, part_of = owner * capacity + row % capacity, row // capacity % 2
    dot = partial(lax.dot_general, dimension_numbers=TOKEN_DOT, preferred_element_type=jnp.float32)
    for head in range(heads):
        taken = slot == target_ref[head]
        own = first_ref[head] + dot(other_ref[head], own_ref[...])
        near = dot(here_ref[head], near_ref[...]) + dot(other_ref[head], far_ref[...])
        padded = jnp.zeros((count, half), jnp.float32)
        for part, grad in enumerate((own, near)):
            high = grad.astype(jnp.bfloat16)
            low = (grad - high.astype(jnp.float32)).astype(jnp.bfloat16)
            pick = jnp.where(taken & (part_of == part), 0.5, 0.0).astype(jnp.bfloat16)
            padded += jnp.dot(
                jnp.concatenate([pick, pick], axis=1),
                jnp.concatenate([high, low], axis=0),
                preferred_element_type=jnp.float32,
            )
        out_ref[:, :, head] = padded.reshape(lines, spots, rows, half)


def padded_gradient(target, cot_here, cot_other, act_here, act_other, lines, spots, capacity):
    heads, tokens, _ = cot_here.shape
    half = act_here[0].shape[1]
    vmem = pl.BlockSpec(memory_space=pltpu.VMEM)
    first = pl.pallas_call(
        first_kernel,
        in_specs=[vmem] * 2,
        out_specs=vmem,
        out_shape=jax.ShapeDtypeStruct((heads, HD, half), jnp.float32),
        compiler_params=PARAMS,
        cost_estimate=cost(2 * heads * tokens * HD * half, 2**20),
    )(cot_here, act_here[0])
    return pl.pallas_call(
        padded_kernel,
        in_specs=[vmem] * 7,
        out_specs=vmem,
        out_shape=jax.ShapeDtypeStruct((lines, spots, heads, 2 * capacity, half), jnp.float32),
        compiler_params=PARAMS,
        cost_estimate=cost(10 * heads * tokens * HD * half, 4 * 2**20),
    )(target[:, None, :], first, cot_here, cot_other, act_other[0], act_here[1], act_other[1])


def placed_part(target_ref, key_ref, rows_ref, cut, span):
    pick = jnp.where(target_ref[...] * CUT + cut == key_ref[...], 1.0, 0.0).astype(jnp.bfloat16)
    return jnp.dot(pick, rows_ref[:, span], preferred_element_type=jnp.float32)


def place_kernel(target_ref, key_ref, rows_ref, out_ref):
    piece = rows_ref.shape[1]
    for cut in range(CUT):
        part = placed_part(target_ref, key_ref, rows_ref, cut, slice(0, piece))
        out_ref[:, cut * piece : (cut + 1) * piece] = part.astype(jnp.bfloat16)


def merge_kernel(target_ref, key_ref, rows_ref, placed_ref, out_ref, parts_ref, sems):
    count, _, part = parts_ref.shape
    copies = []
    for i in range(count):
        place = i * part % rows_ref.shape[1]
        rows = placed_part(
            target_ref, key_ref, rows_ref, i * part // rows_ref.shape[1], slice(place, place + part)
        )
        span = slice(i * part, (i + 1) * part)
        parts_ref[i] = (rows + placed_ref[:, span].astype(jnp.float32)).astype(jnp.bfloat16)
        copies.append(pltpu.make_async_copy(parts_ref.at[i], out_ref.at[:, span], sems.at[i]))
        copies[-1].start()
    for copy in copies:
        copy.wait()


def place_rows(target, key, rows, *placed):
    count, piece = rows.shape
    width, parts = CUT * piece, 2 * CUT
    vmem = pl.BlockSpec(memory_space=pltpu.VMEM)
    scratch = [
        pltpu.VMEM((parts, HD, width // parts), jnp.bfloat16),
        pltpu.SemaphoreType.DMA((parts,)),
    ]
    return pl.pallas_call(
        merge_kernel if placed else place_kernel,
        in_specs=[vmem] * (3 + len(placed)),
        out_specs=pl.BlockSpec(memory_space=pl.ANY) if placed else vmem,
        out_shape=jax.ShapeDtypeStruct((HD, width), jnp.bfloat16),
        scratch_shapes=scratch if placed else [],
        compiler_params=PARAMS,
        cost_estimate=cost(2 * CUT * HD * count * piece, 2 * 2**20),
    )(target, key, rows, *placed)


def body(activations, cotangent, block_start, block_owner, first_moment, block_second, master_rows):
    nx, ny, nc = GRID
    capacity, width = first_moment.shape[2], first_moment.shape[3]
    chips = nx * ny
    core, side, pair = lax.axis_index("c"), lax.axis_index("zl"), lax.axis_index("zh")
    pairs = lax.axis_size("zh")
    chip = lax.axis_index("x") * ny + lax.axis_index("y")
    owner_here = chip * nc + core
    half = activations.shape[1] // 2

    cot_here = copies_to_all(cotangent, "zh")
    def of_side(table):
        return lax.dynamic_index_in_dim(table.reshape(pairs, PAIR, -1), side, 1, keepdims=False)

    target, row_rank = jax.vmap(partial(block_tables, capacity=capacity))(
        of_side(block_start), of_side(block_owner)
    )
    target, activations = lax.optimization_barrier((target, activations))
    keep = lax.dynamic_slice_in_dim(activations, core * half, half, 1)
    give = lax.dynamic_slice_in_dim(activations, (1 - core) * half, half, 1)
    depth = PAIR * pairs
    to_chip = lambda core_to, z: core_to * depth + (z + 2 * core_to - 1) % depth
    same = [(c * depth + z, to_chip(c, z)) for c in range(nc) for z in range(depth)]
    cross = [(c * depth + z, to_chip(1 - c, z)) for c in range(nc) for z in range(depth)]
    act_here = (keep, lax.ppermute(keep, ("c", "zh", "zl"), same))
    far = lax.ppermute(give, ("c", "zh", "zl"), cross)
    cot_here, give = lax.optimization_barrier((cot_here, give))
    act_other = (lax.ppermute(give, "c", SWAP), far)
    cot_other = lax.ppermute(cot_here, "c", SWAP)

    target_here = lax.dynamic_index_in_dim(target, pair, 0, keepdims=False)
    rank_here = lax.dynamic_index_in_dim(row_rank, pair, 0, keepdims=False)
    slot_ids = owner_here * capacity + jnp.arange(capacity, dtype=jnp.int32)
    mine = slot_ids[:, None] == target_here[None, :]
    rank = jnp.max(jnp.where(mine, rank_here[None, :], -1), axis=1)
    row = jnp.arange(chips * capacity * CUT, dtype=jnp.int32)
    from_chip, cut, slot = row // (capacity * CUT), row // capacity % CUT, row % capacity
    key_here = ((from_chip * nc + core) * capacity + slot) * CUT + cut
    key_other = ((from_chip * nc + 1 - core) * capacity + slot) * CUT + cut

    send = padded_gradient(
        target, cot_here, cot_other, act_here, act_other, nx * nc, ny, capacity
    ).astype(jnp.float16)
    send = send.reshape(nx * nc, ny * pairs, 2 * capacity, half)
    send, target_here, rank, key_here, key_other = lax.optimization_barrier(
        (send, target_here[:, None], rank, key_here[None, :], key_other[None, :])
    )
    got = lax.all_to_all(send, ("x", "c"), 0, 0, tiled=True)
    got = got.reshape(nx, nc, ny * pairs, 2 * capacity, half)
    send = jnp.sum(got.astype(jnp.float32), axis=0).astype(jnp.float16)
    got = lax.all_to_all(jnp.swapaxes(send, 0, 1), ("y", "zh"), 0, 0, tiled=True)
    got = got.reshape(ny, pairs, nc, 2, capacity, half)
    summed = jnp.sum(got.astype(jnp.float32), axis=0) * 2.0
    moment, master = first_moment[0, 0], master_rows[0, 0]
    grads, scale, second_new, low = adam_rows(side, rank, summed, moment, block_second[0, 0], master)

    low = copies_to_all(copies_to_all(low.astype(jnp.bfloat16), "y"), "x")
    low = low.reshape(-1, width // CUT)
    low, grads, scale, second_new, target_here, rank = lax.optimization_barrier(
        (low, grads, scale, second_new, target_here, rank)
    )
    filled = (rank >= 0)[:, None]
    moment_new = jnp.where(filled, beta_one * moment + (1.0 - beta_one) * grads, 0.0)
    master_new = master - learn_rate * (moment_new * scale + decay_rate * master)
    master_new = jnp.where(filled, master_new, 0.0)
    low_other = lax.ppermute(low, "c", SWAP)
    placed = place_rows(target_here, key_here, low)
    new_weight = place_rows(target_here, key_other, low_other, placed)
    return (new_weight, moment_new[None, None], second_new[None], master_new[None, None])


def solution(mesh):
    dp, mp = ("x", "y", "c"), ("zh", "zl")
    fine = Mesh(mesh.devices.reshape(GRID + (-1, PAIR)), dp + mp)
    return jax.shard_map(
        body,
        mesh=fine,
        in_specs=(
            P(dp, mp),
            P(dp, mp),
            P(),
            P(),
            P(mp, dp, None, None),
            P(mp, dp, None),
            P(mp, dp, None, None),
        ),
        out_specs=(
            P(mp, None),
            P(mp, dp, None, None),
            P(mp, dp, None),
            P(mp, dp, None, None),
        ),
        check_vma=False,
    )
```

```python
from functools import partial

import jax
import jax.numpy as jnp
from jax import lax
from jax.experimental import pallas as pl
from jax.experimental.pallas import tpu as pltpu
from jax.sharding import Mesh, PartitionSpec as P

HD = 128
GRID = (4, 8, 2)
PAIR = 2
CUT = 2


beta_one = 0.9
beta_two = 0.95
learn_rate = 0.05
decay_rate = 0.1
epsilon = 1e-08
fix_one = 1.0 - 0.9**10
fix_two = 1.0 - 0.95**10


def block_tables(starts, owners, capacity):
    neuron_ids = jnp.arange(HD, dtype=jnp.int32)
    count_blocks = starts.shape[0]
    block_ids = jnp.sum((starts[None, :] <= neuron_ids[:, None]).astype(jnp.int32), axis=1) - 1
    onehot = block_ids[:, None] == jnp.arange(count_blocks, dtype=jnp.int32)[None, :]
    row_owner = jnp.sum(jnp.where(onehot, owners[None, :], 0), axis=1)
    earlier = (row_owner[:, None] == row_owner[None, :]) & (
        neuron_ids[None, :] < neuron_ids[:, None]
    )
    row_slot = jnp.sum(earlier.astype(jnp.int32), axis=1)
    before_blocks = (owners[:, None] == owners[None, :]) & (starts[None, :] < starts[:, None])
    block_rank = jnp.sum(before_blocks.astype(jnp.int32), axis=1)
    row_rank = jnp.sum(jnp.where(onehot, block_rank[None, :], 0), axis=1)
    return row_owner * capacity + row_slot, row_rank


def adam_kernel(side_ref, rank_ref, sums_ref, moment_ref, second_ref, master_ref, *outs):
    grad_out, scale_out, second_out, rows_out = outs
    even = side_ref[0] == 0
    capacity, width = moment_ref.shape
    half = sums_ref.shape[-1]
    blocks = width // (2 * half)
    low = lambda j: sums_ref[j // 2, 0, j % 2]
    high = lambda j: sums_ref[j // 2, 1, 1 - j % 2]
    slots = lax.broadcasted_iota(jnp.int32, (capacity, 1), 0)
    rank = sum(jnp.where(slots == slot, rank_ref[slot], 0) for slot in range(capacity))
    grads = []
    for block in range(blocks):
        grads.append(jnp.where(even, low(block), low((block - 1) % blocks)))
        grads.append(jnp.where(even, high((block + 1) % blocks), high(block)))
    squares = sum(jnp.sum(grad * grad, axis=1, keepdims=True) for grad in grads)
    slot_second = jnp.ones((capacity, 1), jnp.float32)
    for slot in range(2):
        here = rank == slot
        count = jnp.sum(jnp.where(here, float(width), 0.0), axis=0, keepdims=True)
        mean = jnp.sum(jnp.where(here, squares, 0.0), axis=0, keepdims=True) / jnp.maximum(count, 1.0)
        fresh = beta_two * second_ref[:, slot : slot + 1] + (1.0 - beta_two) * mean
        fresh = jnp.where(count > 0.0, fresh, 0.0)
        second_out[:, slot : slot + 1] = fresh
        slot_second = jnp.where(here, fresh, slot_second)
    filled = rank >= 0
    scale = 1.0 / (fix_one * (jnp.sqrt(slot_second / fix_two) + epsilon))
    scale_out[...] = scale
    for part, grad in enumerate(grads):
        span = slice(part * half, (part + 1) * half)
        moment = jnp.where(filled, beta_one * moment_ref[:, span] + (1.0 - beta_one) * grad, 0.0)
        master = master_ref[:, span]
        master = master - learn_rate * (moment * scale + decay_rate * master)
        master = jnp.where(filled, master, 0.0)
        grad_out[:, span] = grad
        piece, place = divmod(part * half, width // CUT)
        rows_out[piece * capacity : (piece + 1) * capacity, place : place + half] = master


def adam_rows(side, rank, sums, moment, second, master):
    capacity, width = moment.shape
    shape = lambda *dims: jax.ShapeDtypeStruct(dims, jnp.float32)
    vmem = pl.BlockSpec(memory_space=pltpu.VMEM)
    return pl.pallas_call(
        adam_kernel,
        in_specs=[pl.BlockSpec(memory_space=pltpu.SMEM)] * 2 + [vmem] * 4,
        out_specs=[vmem] * 4,
        out_shape=[
            shape(capacity, width),
            shape(capacity, 1),
            shape(1, 2),
            shape(capacity * CUT, width // CUT),
        ],
        compiler_params=pltpu.CompilerParams(vmem_limit_bytes=32 * 2**20),
    )(side[None], rank, sums, moment, second[None], master)


SWAP = [(0, 1), (1, 0)]


def copies_to_all(block, axis):
    count = lax.axis_size(axis)
    return lax.all_to_all(jnp.broadcast_to(block[None], (count,) + block.shape), axis, 0, 0, tiled=True)


TOKEN_DOT = (((0,), (0,)), ((), ()))
PARAMS = pltpu.CompilerParams(vmem_limit_bytes=32 * 2**20)


def cost(flops, moved):
    return pl.CostEstimate(flops=flops, bytes_accessed=moved, transcendentals=0)


def first_kernel(cot_ref, act_ref, out_ref):
    for head in range(cot_ref.shape[0]):
        out_ref[head] = lax.dot_general(
            cot_ref[head], act_ref[...], TOKEN_DOT, preferred_element_type=jnp.float32
        )


def padded_kernel(target_ref, first_ref, here_ref, other_ref, near_ref, far_ref, own_ref, out_ref):
    lines, spots, heads, rows, half = out_ref.shape
    count, cores, capacity = lines * spots * rows, GRID[2], rows // 2
    row = lax.broadcasted_iota(jnp.int32, (count, HD), 0)
    line, spot = row // (spots * rows), row // rows % spots
    owner = (line // cores * spots + spot) * cores + line % cores
    slot, part_of = owner * capacity + row % capacity, row // capacity % 2
    dot = partial(lax.dot_general, dimension_numbers=TOKEN_DOT, preferred_element_type=jnp.float32)
    for head in range(heads):
        taken = slot == target_ref[head]
        own = first_ref[head] + dot(other_ref[head], own_ref[...])
        near = dot(here_ref[head], near_ref[...]) + dot(other_ref[head], far_ref[...])
        padded = jnp.zeros((count, half), jnp.float32)
        for part, grad in enumerate((own, near)):
            high = grad.astype(jnp.bfloat16)
            low = (grad - high.astype(jnp.float32)).astype(jnp.bfloat16)
            pick = jnp.where(taken & (part_of == part), 0.5, 0.0).astype(jnp.bfloat16)
            padded += jnp.dot(
                jnp.concatenate([pick, pick], axis=1),
                jnp.concatenate([high, low], axis=0),
                preferred_element_type=jnp.float32,
            )
        out_ref[:, :, head] = padded.reshape(lines, spots, rows, half)


def padded_gradient(target, cot_here, cot_other, act_here, act_other, lines, spots, capacity):
    heads, tokens, _ = cot_here.shape
    half = act_here[0].shape[1]
    vmem = pl.BlockSpec(memory_space=pltpu.VMEM)
    first = pl.pallas_call(
        first_kernel,
        in_specs=[vmem] * 2,
        out_specs=vmem,
        out_shape=jax.ShapeDtypeStruct((heads, HD, half), jnp.float32),
        compiler_params=PARAMS,
        cost_estimate=cost(2 * heads * tokens * HD * half, 2**20),
    )(cot_here, act_here[0])
    return pl.pallas_call(
        padded_kernel,
        in_specs=[vmem] * 7,
        out_specs=vmem,
        out_shape=jax.ShapeDtypeStruct((lines, spots, heads, 2 * capacity, half), jnp.float32),
        compiler_params=PARAMS,
        cost_estimate=cost(10 * heads * tokens * HD * half, 4 * 2**20),
    )(target[:, None, :], first, cot_here, cot_other, act_here[1], act_other[1], act_other[0])


def placed_part(target_ref, key_ref, rows_ref, cut, span):
    pick = jnp.where(target_ref[...] * CUT + cut == key_ref[...], 1.0, 0.0).astype(jnp.bfloat16)
    return jnp.dot(pick, rows_ref[:, span], preferred_element_type=jnp.float32)


def place_kernel(target_ref, key_ref, rows_ref, out_ref):
    piece = rows_ref.shape[1]
    for cut in range(CUT):
        part = placed_part(target_ref, key_ref, rows_ref, cut, slice(0, piece))
        out_ref[:, cut * piece : (cut + 1) * piece] = part.astype(jnp.bfloat16)


def merge_kernel(target_ref, key_ref, rows_ref, placed_ref, out_ref, parts_ref, sems):
    count, _, part = parts_ref.shape
    copies = []
    for i in range(count):
        place = i * part % rows_ref.shape[1]
        rows = placed_part(
            target_ref, key_ref, rows_ref, i * part // rows_ref.shape[1], slice(place, place + part)
        )
        span = slice(i * part, (i + 1) * part)
        parts_ref[i] = (rows + placed_ref[:, span].astype(jnp.float32)).astype(jnp.bfloat16)
        copies.append(pltpu.make_async_copy(parts_ref.at[i], out_ref.at[:, span], sems.at[i]))
        copies[-1].start()
    for copy in copies:
        copy.wait()


def place_rows(target, key, rows, *placed):
    count, piece = rows.shape
    width, parts = CUT * piece, 2 * CUT
    vmem = pl.BlockSpec(memory_space=pltpu.VMEM)
    scratch = [
        pltpu.VMEM((parts, HD, width // parts), jnp.bfloat16),
        pltpu.SemaphoreType.DMA((parts,)),
    ]
    return pl.pallas_call(
        merge_kernel if placed else place_kernel,
        in_specs=[vmem] * (3 + len(placed)),
        out_specs=pl.BlockSpec(memory_space=pl.ANY) if placed else vmem,
        out_shape=jax.ShapeDtypeStruct((HD, width), jnp.bfloat16),
        scratch_shapes=scratch if placed else [],
        compiler_params=PARAMS,
        cost_estimate=cost(2 * CUT * HD * count * piece, 2 * 2**20),
    )(target, key, rows, *placed)


def body(activations, cotangent, block_start, block_owner, first_moment, block_second, master_rows):
    nx, ny, nc = GRID
    capacity, width = first_moment.shape[2], first_moment.shape[3]
    chips = nx * ny
    core, side, pair = lax.axis_index("c"), lax.axis_index("zl"), lax.axis_index("zh")
    pairs = lax.axis_size("zh")
    chip = lax.axis_index("x") * ny + lax.axis_index("y")
    owner_here = chip * nc + core
    half = activations.shape[1] // 2

    cot_here = copies_to_all(cotangent, "zh")
    def of_side(table):
        return lax.dynamic_index_in_dim(table.reshape(pairs, PAIR, -1), side, 1, keepdims=False)

    target, row_rank = jax.vmap(partial(block_tables, capacity=capacity))(
        of_side(block_start), of_side(block_owner)
    )
    target, activations = lax.optimization_barrier((target, activations))
    keep = lax.dynamic_slice_in_dim(activations, core * half, half, 1)
    give = lax.dynamic_slice_in_dim(activations, (1 - core) * half, half, 1)
    depth = PAIR * pairs
    to_chip = lambda core_to, z: core_to * depth + (z + 2 * core_to - 1) % depth
    same = [(c * depth + z, to_chip(c, z)) for c in range(nc) for z in range(depth)]
    cross = [(c * depth + z, to_chip(1 - c, z)) for c in range(nc) for z in range(depth)]
    act_here = (keep, lax.ppermute(keep, ("c", "zh", "zl"), same))
    act_other = (lax.ppermute(give, "c", SWAP), lax.ppermute(give, ("c", "zh", "zl"), cross))
    cot_other = lax.ppermute(cot_here, "c", SWAP)

    target_here = lax.dynamic_index_in_dim(target, pair, 0, keepdims=False)
    rank_here = lax.dynamic_index_in_dim(row_rank, pair, 0, keepdims=False)
    slot_ids = owner_here * capacity + jnp.arange(capacity, dtype=jnp.int32)
    mine = slot_ids[:, None] == target_here[None, :]
    rank = jnp.max(jnp.where(mine, rank_here[None, :], -1), axis=1)
    row = jnp.arange(chips * capacity * CUT, dtype=jnp.int32)
    from_chip, cut, slot = row // (capacity * CUT), row // capacity % CUT, row % capacity
    key_here = ((from_chip * nc + core) * capacity + slot) * CUT + cut
    key_other = ((from_chip * nc + 1 - core) * capacity + slot) * CUT + cut

    send = padded_gradient(
        target, cot_here, cot_other, act_here, act_other, nx * nc, ny, capacity
    ).astype(jnp.float16)
    send = send.reshape(nx * nc, ny * pairs, 2 * capacity, half)
    send, target_here, rank, key_here, key_other = lax.optimization_barrier(
        (send, target_here[:, None], rank, key_here[None, :], key_other[None, :])
    )
    got = lax.all_to_all(send, ("x", "c"), 0, 0, tiled=True)
    got = got.reshape(nx, nc, ny * pairs, 2 * capacity, half)
    send = jnp.sum(got.astype(jnp.float32), axis=0).astype(jnp.float16)
    got = lax.all_to_all(jnp.swapaxes(send, 0, 1), ("y", "zh"), 0, 0, tiled=True)
    got = got.reshape(ny, pairs, nc, 2, capacity, half)
    summed = jnp.sum(got.astype(jnp.float32), axis=0) * 2.0
    moment, master = first_moment[0, 0], master_rows[0, 0]
    grads, scale, second_new, low = adam_rows(side, rank, summed, moment, block_second[0, 0], master)

    low = copies_to_all(copies_to_all(low.astype(jnp.bfloat16), "y"), "x")
    low = low.reshape(-1, width // CUT)
    low, grads, scale, second_new, target_here, rank = lax.optimization_barrier(
        (low, grads, scale, second_new, target_here, rank)
    )
    filled = (rank >= 0)[:, None]
    moment_new = jnp.where(filled, beta_one * moment + (1.0 - beta_one) * grads, 0.0)
    master_new = master - learn_rate * (moment_new * scale + decay_rate * master)
    master_new = jnp.where(filled, master_new, 0.0)
    low_other = lax.ppermute(low, "c", SWAP)
    placed = place_rows(target_here, key_here, low)
    new_weight = place_rows(target_here, key_other, low_other, placed)
    return (new_weight, moment_new[None, None], second_new[None], master_new[None, None])


def solution(mesh):
    dp, mp = ("x", "y", "c"), ("zh", "zl")
    fine = Mesh(mesh.devices.reshape(GRID + (-1, PAIR)), dp + mp)
    return jax.shard_map(
        body,
        mesh=fine,
        in_specs=(
            P(dp, mp),
            P(dp, mp),
            P(),
            P(),
            P(mp, dp, None, None),
            P(mp, dp, None),
            P(mp, dp, None, None),
        ),
        out_specs=(
            P(mp, None),
            P(mp, dp, None, None),
            P(mp, dp, None),
            P(mp, dp, None, None),
        ),
        check_vma=False,
    )
```

```python
from functools import partial

import jax
import jax.numpy as jnp
from jax import lax
from jax.experimental import pallas as pl
from jax.experimental.pallas import tpu as pltpu
from jax.sharding import Mesh, PartitionSpec as P

HD = 128
GRID = (4, 8, 2)
PAIR = 2
CUT = 2


beta_one = 0.9
beta_two = 0.95
learn_rate = 0.05
decay_rate = 0.1
epsilon = 1e-08
fix_one = 1.0 - 0.9**10
fix_two = 1.0 - 0.95**10


def block_tables(starts, owners, capacity):
    neuron_ids = jnp.arange(HD, dtype=jnp.int32)
    count_blocks = starts.shape[0]
    block_ids = jnp.sum((starts[None, :] <= neuron_ids[:, None]).astype(jnp.int32), axis=1) - 1
    onehot = block_ids[:, None] == jnp.arange(count_blocks, dtype=jnp.int32)[None, :]
    row_owner = jnp.sum(jnp.where(onehot, owners[None, :], 0), axis=1)
    earlier = (row_owner[:, None] == row_owner[None, :]) & (
        neuron_ids[None, :] < neuron_ids[:, None]
    )
    row_slot = jnp.sum(earlier.astype(jnp.int32), axis=1)
    before_blocks = (owners[:, None] == owners[None, :]) & (starts[None, :] < starts[:, None])
    block_rank = jnp.sum(before_blocks.astype(jnp.int32), axis=1)
    row_rank = jnp.sum(jnp.where(onehot, block_rank[None, :], 0), axis=1)
    return row_owner * capacity + row_slot, row_rank


def adam_kernel(side_ref, rank_ref, sums_ref, moment_ref, second_ref, master_ref, *outs):
    grad_out, scale_out, second_out, rows_out = outs
    even = side_ref[0] == 0
    capacity, width = moment_ref.shape
    half = sums_ref.shape[-1]
    blocks = width // (2 * half)
    low = lambda j: sums_ref[j // 2, 0, j % 2]
    high = lambda j: sums_ref[j // 2, 1, 1 - j % 2]
    slots = lax.broadcasted_iota(jnp.int32, (capacity, 1), 0)
    rank = sum(jnp.where(slots == slot, rank_ref[slot], 0) for slot in range(capacity))
    grads = []
    for block in range(blocks):
        grads.append(jnp.where(even, low(block), low((block - 1) % blocks)))
        grads.append(jnp.where(even, high((block + 1) % blocks), high(block)))
    squares = sum(jnp.sum(grad * grad, axis=1, keepdims=True) for grad in grads)
    slot_second = jnp.ones((capacity, 1), jnp.float32)
    for slot in range(2):
        here = rank == slot
        count = jnp.sum(jnp.where(here, float(width), 0.0), axis=0, keepdims=True)
        mean = jnp.sum(jnp.where(here, squares, 0.0), axis=0, keepdims=True) / jnp.maximum(count, 1.0)
        fresh = beta_two * second_ref[:, slot : slot + 1] + (1.0 - beta_two) * mean
        fresh = jnp.where(count > 0.0, fresh, 0.0)
        second_out[:, slot : slot + 1] = fresh
        slot_second = jnp.where(here, fresh, slot_second)
    filled = rank >= 0
    scale = 1.0 / (fix_one * (jnp.sqrt(slot_second / fix_two) + epsilon))
    scale_out[...] = scale
    for part, grad in enumerate(grads):
        span = slice(part * half, (part + 1) * half)
        moment = jnp.where(filled, beta_one * moment_ref[:, span] + (1.0 - beta_one) * grad, 0.0)
        master = master_ref[:, span]
        master = master - learn_rate * (moment * scale + decay_rate * master)
        master = jnp.where(filled, master, 0.0)
        grad_out[:, span] = grad
        piece, place = divmod(part * half, width // CUT)
        rows_out[piece * capacity : (piece + 1) * capacity, place : place + half] = master


def adam_rows(side, rank, sums, moment, second, master):
    capacity, width = moment.shape
    shape = lambda *dims: jax.ShapeDtypeStruct(dims, jnp.float32)
    vmem = pl.BlockSpec(memory_space=pltpu.VMEM)
    return pl.pallas_call(
        adam_kernel,
        in_specs=[pl.BlockSpec(memory_space=pltpu.SMEM)] * 2 + [vmem] * 4,
        out_specs=[vmem] * 4,
        out_shape=[
            shape(capacity, width),
            shape(capacity, 1),
            shape(1, 2),
            shape(capacity * CUT, width // CUT),
        ],
        compiler_params=pltpu.CompilerParams(vmem_limit_bytes=32 * 2**20),
    )(side[None], rank, sums, moment, second[None], master)


SWAP = [(0, 1), (1, 0)]


def copies_to_all(block, axis):
    count = lax.axis_size(axis)
    return lax.all_to_all(jnp.broadcast_to(block[None], (count,) + block.shape), axis, 0, 0, tiled=True)


TOKEN_DOT = (((0,), (0,)), ((), ()))
PARAMS = pltpu.CompilerParams(vmem_limit_bytes=32 * 2**20)


def cost(flops, moved):
    return pl.CostEstimate(flops=flops, bytes_accessed=moved, transcendentals=0)


def first_kernel(cot_ref, act_ref, out_ref):
    for head in range(cot_ref.shape[0]):
        out_ref[head] = lax.dot_general(
            cot_ref[head], act_ref[...], TOKEN_DOT, preferred_element_type=jnp.float32
        )


def padded_kernel(target_ref, first_ref, here_ref, other_ref, own_ref, near_ref, far_ref, out_ref):
    lines, spots, heads, rows, half = out_ref.shape
    count, cores, capacity = lines * spots * rows, GRID[2], rows // 2
    row = lax.broadcasted_iota(jnp.int32, (count, HD), 0)
    line, spot = row // (spots * rows), row // rows % spots
    owner = (line // cores * spots + spot) * cores + line % cores
    slot, part_of = owner * capacity + row % capacity, row // capacity % 2
    dot = partial(lax.dot_general, dimension_numbers=TOKEN_DOT, preferred_element_type=jnp.float32)
    for head in range(heads):
        taken = slot == target_ref[head]
        own = first_ref[head] + dot(other_ref[head], own_ref[...])
        near = dot(here_ref[head], near_ref[...]) + dot(other_ref[head], far_ref[...])
        padded = jnp.zeros((count, half), jnp.float32)
        for part, grad in enumerate((own, near)):
            high = grad.astype(jnp.bfloat16)
            low = (grad - high.astype(jnp.float32)).astype(jnp.bfloat16)
            pick = jnp.where(taken & (part_of == part), 0.5, 0.0).astype(jnp.bfloat16)
            padded += jnp.dot(
                jnp.concatenate([pick, pick], axis=1),
                jnp.concatenate([high, low], axis=0),
                preferred_element_type=jnp.float32,
            )
        out_ref[:, :, head] = padded.reshape(lines, spots, rows, half)


def padded_gradient(target, cot_here, cot_other, act_here, act_other, lines, spots, capacity):
    heads, tokens, _ = cot_here.shape
    half = act_here[0].shape[1]
    vmem = pl.BlockSpec(memory_space=pltpu.VMEM)
    first = pl.pallas_call(
        first_kernel,
        in_specs=[vmem] * 2,
        out_specs=vmem,
        out_shape=jax.ShapeDtypeStruct((heads, HD, half), jnp.float32),
        compiler_params=PARAMS,
        cost_estimate=cost(2 * heads * tokens * HD * half, 2**20),
    )(cot_here, act_here[0])
    return pl.pallas_call(
        padded_kernel,
        in_specs=[vmem] * 7,
        out_specs=vmem,
        out_shape=jax.ShapeDtypeStruct((lines, spots, heads, 2 * capacity, half), jnp.float32),
        compiler_params=PARAMS,
        cost_estimate=cost(10 * heads * tokens * HD * half, 4 * 2**20),
    )(target[:, None, :], first, cot_here, cot_other, act_other[0], act_here[1], act_other[1])


def placed_part(target_ref, key_ref, rows_ref, cut, span):
    pick = jnp.where(target_ref[...] * CUT + cut == key_ref[...], 1.0, 0.0).astype(jnp.bfloat16)
    return jnp.dot(pick, rows_ref[:, span], preferred_element_type=jnp.float32)


def place_kernel(target_ref, key_ref, rows_ref, out_ref):
    piece = rows_ref.shape[1]
    for cut in range(CUT):
        part = placed_part(target_ref, key_ref, rows_ref, cut, slice(0, piece))
        out_ref[:, cut * piece : (cut + 1) * piece] = part.astype(jnp.bfloat16)


def merge_kernel(target_ref, key_ref, rows_ref, placed_ref, out_ref, parts_ref, sems):
    count, _, part = parts_ref.shape
    copies = []
    for i in range(count):
        place = i * part % rows_ref.shape[1]
        rows = placed_part(
            target_ref, key_ref, rows_ref, i * part // rows_ref.shape[1], slice(place, place + part)
        )
        span = slice(i * part, (i + 1) * part)
        parts_ref[i] = (rows + placed_ref[:, span].astype(jnp.float32)).astype(jnp.bfloat16)
        copies.append(pltpu.make_async_copy(parts_ref.at[i], out_ref.at[:, span], sems.at[i]))
        copies[-1].start()
    for copy in copies:
        copy.wait()


def place_rows(target, key, rows, *placed):
    count, piece = rows.shape
    width, parts = CUT * piece, 4 * CUT
    vmem = pl.BlockSpec(memory_space=pltpu.VMEM)
    scratch = [
        pltpu.VMEM((parts, HD, width // parts), jnp.bfloat16),
        pltpu.SemaphoreType.DMA((parts,)),
    ]
    return pl.pallas_call(
        merge_kernel if placed else place_kernel,
        in_specs=[vmem] * (3 + len(placed)),
        out_specs=pl.BlockSpec(memory_space=pl.ANY) if placed else vmem,
        out_shape=jax.ShapeDtypeStruct((HD, width), jnp.bfloat16),
        scratch_shapes=scratch if placed else [],
        compiler_params=PARAMS,
        cost_estimate=cost(2 * CUT * HD * count * piece, 2 * 2**20),
    )(target, key, rows, *placed)


def body(activations, cotangent, block_start, block_owner, first_moment, block_second, master_rows):
    nx, ny, nc = GRID
    capacity, width = first_moment.shape[2], first_moment.shape[3]
    chips = nx * ny
    core, side, pair = lax.axis_index("c"), lax.axis_index("zl"), lax.axis_index("zh")
    pairs = lax.axis_size("zh")
    chip = lax.axis_index("x") * ny + lax.axis_index("y")
    owner_here = chip * nc + core
    half = activations.shape[1] // 2

    cot_here = copies_to_all(cotangent, "zh")
    def of_side(table):
        return lax.dynamic_index_in_dim(table.reshape(pairs, PAIR, -1), side, 1, keepdims=False)

    target, row_rank = jax.vmap(partial(block_tables, capacity=capacity))(
        of_side(block_start), of_side(block_owner)
    )
    target, activations = lax.optimization_barrier((target, activations))
    keep = lax.dynamic_slice_in_dim(activations, core * half, half, 1)
    give = lax.dynamic_slice_in_dim(activations, (1 - core) * half, half, 1)
    depth = PAIR * pairs
    to_chip = lambda core_to, z: core_to * depth + (z + 2 * core_to - 1) % depth
    same = [(c * depth + z, to_chip(c, z)) for c in range(nc) for z in range(depth)]
    cross = [(c * depth + z, to_chip(1 - c, z)) for c in range(nc) for z in range(depth)]
    act_here = (keep, lax.ppermute(keep, ("c", "zh", "zl"), same))
    act_other = (lax.ppermute(give, "c", SWAP), lax.ppermute(give, ("c", "zh", "zl"), cross))
    cot_other = lax.ppermute(cot_here, "c", SWAP)

    target_here = lax.dynamic_index_in_dim(target, pair, 0, keepdims=False)
    rank_here = lax.dynamic_index_in_dim(row_rank, pair, 0, keepdims=False)
    slot_ids = owner_here * capacity + jnp.arange(capacity, dtype=jnp.int32)
    mine = slot_ids[:, None] == target_here[None, :]
    rank = jnp.max(jnp.where(mine, rank_here[None, :], -1), axis=1)
    row = jnp.arange(chips * capacity * CUT, dtype=jnp.int32)
    from_chip, cut, slot = row // (capacity * CUT), row // capacity % CUT, row % capacity
    key_here = ((from_chip * nc + core) * capacity + slot) * CUT + cut
    key_other = ((from_chip * nc + 1 - core) * capacity + slot) * CUT + cut

    send = padded_gradient(
        target, cot_here, cot_other, act_here, act_other, nx * nc, ny, capacity
    ).astype(jnp.float16)
    send = send.reshape(nx * nc, ny * pairs, 2 * capacity, half)
    send, target_here, rank, key_here, key_other = lax.optimization_barrier(
        (send, target_here[:, None], rank, key_here[None, :], key_other[None, :])
    )
    got = lax.all_to_all(send, ("x", "c"), 0, 0, tiled=True)
    got = got.reshape(nx, nc, ny * pairs, 2 * capacity, half)
    send = jnp.sum(got.astype(jnp.float32), axis=0).astype(jnp.float16)
    got = lax.all_to_all(jnp.swapaxes(send, 0, 1), ("y", "zh"), 0, 0, tiled=True)
    got = got.reshape(ny, pairs, nc, 2, capacity, half)
    summed = jnp.sum(got.astype(jnp.float32), axis=0) * 2.0
    moment, master = first_moment[0, 0], master_rows[0, 0]
    grads, scale, second_new, low = adam_rows(side, rank, summed, moment, block_second[0, 0], master)

    low = copies_to_all(copies_to_all(low.astype(jnp.bfloat16), "y"), "x")
    low = low.reshape(-1, width // CUT)
    low, grads, scale, second_new, target_here, rank = lax.optimization_barrier(
        (low, grads, scale, second_new, target_here, rank)
    )
    filled = (rank >= 0)[:, None]
    moment_new = jnp.where(filled, beta_one * moment + (1.0 - beta_one) * grads, 0.0)
    master_new = master - learn_rate * (moment_new * scale + decay_rate * master)
    master_new = jnp.where(filled, master_new, 0.0)
    low_other = lax.ppermute(low, "c", SWAP)
    placed = place_rows(target_here, key_here, low)
    new_weight = place_rows(target_here, key_other, low_other, placed)
    return (new_weight, moment_new[None, None], second_new[None], master_new[None, None])


def solution(mesh):
    dp, mp = ("x", "y", "c"), ("zh", "zl")
    fine = Mesh(mesh.devices.reshape(GRID + (-1, PAIR)), dp + mp)
    return jax.shard_map(
        body,
        mesh=fine,
        in_specs=(
            P(dp, mp),
            P(dp, mp),
            P(),
            P(),
            P(mp, dp, None, None),
            P(mp, dp, None),
            P(mp, dp, None, None),
        ),
        out_specs=(
            P(mp, None),
            P(mp, dp, None, None),
            P(mp, dp, None),
            P(mp, dp, None, None),
        ),
        check_vma=False,
    )
```
